256 devices in a mesh: critic: 16 (over y, z_hi, core), seq: 4 (over x), tensor: 4 (over z_lo).
Axes of the slice: x: 4, y: 4, z: 8 (z_hi: 2, z_lo: 4; z = z_hi * 4 + z_lo), core: 2. Of those that a mesh axis runs over, the one named last changes fastest.
Arguments:
- observations: bfloat16 [16, 256, 2048], P('seq', 'critic', 'tensor'), may hold values from -6 to 6
- actions: bfloat16 [16, 384], P('seq', 'critic'), may hold values from -6 to 6
- lengths: int32 [16], P('seq'), may hold values from 1 to 256, as said below
- boot_mask: int32 [16, 16], P('critic', 'seq'), may hold values 0 or 1
- project_weight: bfloat16 [16, 2048, 3, 2048], P('critic', None, None, 'tensor'), may hold values from -0.125 to 0.125
- output_weight: bfloat16 [16, 2048, 2048], P('critic', 'tensor'), may hold values from -0.125 to 0.125
- action_weight: bfloat16 [16, 384, 2048], P('critic'), may hold values from -0.3125 to 0.3125
- norm_gain: float32 [16, 2048], P('critic'), may hold values from 0.5 to 1.5
- value_head: float32 [16, 2048], P('critic'), may hold values from -0.6 to 0.6
Outputs:
- q_values: float32 [16, 16], P('critic', 'seq')
- obs_grad: float32 [16, 256, 2048], P('seq', 'critic', 'tensor')
- action_grad: float32 [16, 384], P('seq', ('critic', 'tensor'))
The draws below stay inside these ranges and needn't reach their ends.
Inputs may be any that keep to these rules, and one draw needn't show every extreme that they name: `lengths`: each sequence's number of valid history steps; later positions are padding.
All inputs are finite; a program needn't handle non-finite values. No bound on the sum of `boot_mask` on one device may be relied on, other than what follows from the above.
Results may differ from the reference program's by a relative error of at most 0.0065.
Values may be sent and summed in bfloat16 or wider, within the bound.
A program may use at most 128 MiB of HBM per device.

```python
import jax
import jax.numpy as jnp
from jax import lax

D = 2048
HEADS = 16
HEAD_DIM = 128
HIST = 256
ACT = 384
CRITICS = 16
SEQS = 16


def draw_lengths(key, part):
    key = jax.random.fold_in(key, 7)
    drawn = jax.random.randint(key, (SEQS,), 1, HIST + 1)
    return drawn.at[0].set(HIST).astype(jnp.int32)


def set_ends(entries, rng, low, high):
    extent = entries.shape
    index_at = [jax.random.randint(jax.random.fold_in(rng, axis), (), 0, extent[axis]) for axis in range(len(extent))]
    entries = entries.at[tuple(index_at)].set(low)
    longest = extent.index(max(extent))
    index_at[longest] = (index_at[longest] + 1) % extent[longest]
    return entries.at[tuple(index_at)].set(high)


def level_of(rng, dims, cuts, low, largest):
    loudness = 1.0
    for axis_at, parts in cuts:
        heights = jax.random.uniform(jax.random.fold_in(jax.random.fold_in(rng, 6), axis_at), (parts,), jnp.float32, low / len(cuts), largest / len(cuts))
        loudness = loudness * jnp.repeat(jnp.exp(heights), dims[axis_at] // parts).reshape((-1,) + (1,) * (len(dims) - 1 - axis_at))
    return loudness


def normal_values(rng, extent, deviation, reach, cuts=(), held_as=jnp.bfloat16):
    factor_of = level_of(rng, extent, cuts, -0.22, 0.18) if cuts else 1.0
    values = jax.random.normal(rng, extent, jnp.float32) * deviation * factor_of
    return jnp.minimum(jnp.maximum(values, -reach), reach).astype(held_as)


def setup_inputs(seed: int = 0) -> dict:
    seeds = jax.random.split(jax.random.key(seed), 10)
    return {
        "observations": normal_values(seeds[0], (SEQS, HIST, D), 1.0, 6.0, ((0, 4), (1, 16), (2, 4))),
        "actions": normal_values(seeds[1], (SEQS, ACT), 1.0, 6.0, ((0, 4), (1, 16))),
        "lengths": draw_lengths(jax.random.fold_in(seeds[9], 71), 0),
        "boot_mask": set_ends((jax.random.randint(seeds[3], (CRITICS, SEQS), 0, 2) < 1).astype(jnp.int32), jax.random.fold_in(seeds[3], 1), 0, 1),
        "project_weight": normal_values(seeds[4], (CRITICS, D, 3, HEADS * HEAD_DIM), D ** -0.5, 0.125, ((0, 16), (3, 4))),
        "output_weight": normal_values(seeds[5], (CRITICS, HEADS * HEAD_DIM, D), (HEADS * HEAD_DIM) ** -0.5, 0.125, ((0, 16), (1, 4))),
        "action_weight": normal_values(seeds[6], (CRITICS, ACT, D), ACT ** -0.5, 0.3125, ((0, 16),)),
        "norm_gain": jnp.clip(1.0 + 0.1 * jax.random.normal(seeds[7], (CRITICS, D), jnp.float32), 0.5, 1.5),
        "value_head": normal_values(seeds[8], (CRITICS, D), 0.1, 0.6, ((0, 16),), jnp.float32),
    }


highest = lax.Precision.HIGHEST
norm_eps = 1e-05

def attend(query_vec, key_rows, value_rows, is_valid):
    scores = jnp.einsum('shd,slhd->shl', query_vec, key_rows.astype(jnp.float32), precision=highest) * HEAD_DIM ** (-0.5)
    scores = jnp.where(is_valid[:, None, :], scores, -1e+30)
    attention = jax.nn.softmax(scores, axis=-1)
    attention_round = attention.astype(jnp.bfloat16)
    attended = jnp.einsum('shl,slhd->shd', attention_round.astype(jnp.float32), value_rows.astype(jnp.float32), precision=highest)
    return (attention, attention_round, attended.astype(jnp.bfloat16).reshape(query_vec.shape[0], -1))

def attend_back(grad_heads, query_vec, key_rows, value_rows, attention, attention_round):
    value_float = value_rows.astype(jnp.float32)
    key_float = key_rows.astype(jnp.float32)
    grad_attention = jnp.einsum('shd,slhd->shl', grad_heads, value_float, precision=highest)
    grad_value = jnp.einsum('shl,shd->slhd', attention_round.astype(jnp.float32), grad_heads, precision=highest)
    grad_scores = attention * (grad_attention - lax.optimization_barrier(jnp.sum(attention * grad_attention, axis=-1, keepdims=True)))
    grad_query = jnp.einsum('shl,slhd->shd', grad_scores, key_float, precision=highest) * HEAD_DIM ** (-0.5)
    grad_key = jnp.einsum('shl,shd->slhd', grad_scores, query_vec, precision=highest) * HEAD_DIM ** (-0.5)
    return (grad_query, grad_key, grad_value)

def head_forward(hidden_last, gain_row, head_row):
    inverse = lax.rsqrt(lax.optimization_barrier(jnp.mean(hidden_last * hidden_last, axis=-1, keepdims=True)) + norm_eps)
    normed = hidden_last * inverse
    return (lax.optimization_barrier(jnp.sum(head_row * gain_row * normed, axis=-1)), normed, inverse)

def head_backward(weight_row, normed, inverse, gain_row, head_row):
    grad_normed = weight_row[:, None] * head_row * gain_row
    return inverse * (grad_normed - normed * lax.optimization_barrier(jnp.mean(grad_normed * normed, axis=-1, keepdims=True)))

def critic_pass(observations, actions, lengths, weight_row, project, out_weight, act_weight, gain_row, head_row):
    count_seq, length_hist, model_width = observations.shape
    inner_width = project.shape[2]
    head_count = inner_width // HEAD_DIM
    last_pos = (lengths - 1).astype(jnp.int32)
    row_ids = jnp.arange(count_seq, dtype=jnp.int32)
    positions = jnp.arange(length_hist, dtype=jnp.int32)
    is_last = positions[None, :] == last_pos[:, None]
    is_valid = positions[None, :] < lengths[:, None]
    query_weight = project[:, 0]
    keyval_weight = project[:, 1:].reshape(model_width, 2 * inner_width)
    embedded = jnp.dot(actions, act_weight, preferred_element_type=jnp.float32)
    last_row = observations[row_ids, last_pos].astype(jnp.float32) + embedded
    last_round = last_row.astype(jnp.bfloat16)
    mixed = jnp.where(is_last[:, :, None], last_round[:, None, :], observations)
    keyval_rows = jnp.dot(mixed.reshape(-1, model_width), keyval_weight, preferred_element_type=jnp.float32).astype(jnp.bfloat16)
    keyval_rows = keyval_rows.reshape(count_seq, length_hist, 2 * inner_width)
    key_rows = keyval_rows[:, :, :inner_width].reshape(count_seq, length_hist, head_count, HEAD_DIM)
    value_rows = keyval_rows[:, :, inner_width:].reshape(count_seq, length_hist, head_count, HEAD_DIM)
    query_vec = jnp.dot(last_round, query_weight, preferred_element_type=jnp.float32).reshape(count_seq, head_count, HEAD_DIM)
    attention, attention_round, attended = attend(query_vec, key_rows, value_rows, is_valid)
    hidden_last = last_row + jnp.dot(attended, out_weight, preferred_element_type=jnp.float32)
    q_vals, normed, inverse = head_forward(hidden_last, gain_row, head_row)
    grad_last = head_backward(weight_row, normed, inverse, gain_row, head_row)
    grad_heads = jnp.dot(grad_last, out_weight.T, precision=highest, preferred_element_type=jnp.float32)
    grad_heads = grad_heads.reshape(count_seq, head_count, HEAD_DIM)
    grad_query, grad_key, grad_value = attend_back(grad_heads, query_vec, key_rows, value_rows, attention, attention_round)
    grad_keyval = jnp.concatenate([grad_key.reshape(-1, inner_width), grad_value.reshape(-1, inner_width)], axis=1).astype(jnp.bfloat16)
    grad_mixed = jnp.dot(grad_keyval, keyval_weight.T, preferred_element_type=jnp.float32).reshape(count_seq, length_hist, model_width)
    grad_lastrow = grad_last + jnp.dot(grad_query.reshape(count_seq, inner_width), query_weight.T, precision=highest, preferred_element_type=jnp.float32)
    grad_lastrow = grad_lastrow + grad_mixed[row_ids, last_pos]
    grad_rows = jnp.where(is_last[:, :, None], grad_lastrow[:, None, :], grad_mixed)
    grad_acts = jnp.dot(grad_lastrow, act_weight.T, precision=highest, preferred_element_type=jnp.float32)
    return (q_vals, grad_rows, grad_acts)

def reference(observations, actions, lengths, boot_mask, project_weight, output_weight, action_weight, norm_gain, value_head):

    def member_pass(carry, member):
        mask_row, project, out_weight, act_weight, gain_row, head_row = member
        q_vals, grad_rows, grad_acts = critic_pass(observations, actions, lengths, mask_row.astype(jnp.float32), project, out_weight, act_weight, gain_row, head_row)
        return ((carry[0] + grad_rows, carry[1] + grad_acts), q_vals)
    initial = (jnp.zeros(observations.shape, jnp.float32), jnp.zeros(actions.shape, jnp.float32))
    totals, q_values = lax.scan(member_pass, initial, (boot_mask, project_weight, output_weight, action_weight, norm_gain, value_head))
    return (q_values, totals[0], totals[1])
```

```python
import functools

import jax
import jax.numpy as jnp
from jax import lax
from jax.experimental import pallas as pl
from jax.experimental.pallas import tpu as pltpu
from jax.sharding import PartitionSpec as P

HEAD_DIM = 128
NORM_EPS = 1e-05
CORES = 2
HALVES = 2

f32 = jnp.float32
bf16 = jnp.bfloat16
NN = (((1,), (0,)), ((), ()))
NT_DIMS = (((1,), (1,)), ((), ()))


def mod(value, count):
    return lax.rem(value + count, count)


def iota(shape, axis):
    return lax.broadcasted_iota(jnp.int32, shape, axis)


def split(x):
    high = x.astype(bf16).astype(f32)
    return jnp.concatenate([high, x - high], axis=0).astype(bf16)


def dot(x, w, dims=NN):
    return lax.dot_general(x, w, dims, preferred_element_type=f32)


def dot_split(x, w, dims=NN):
    rows = x.shape[0]
    both = dot(split(x), w, dims)
    return both[:rows] + both[rows:]


def dot_exact(x, w):
    rows = x.shape[0]
    high = x.astype(bf16).astype(f32)
    rest = x - high
    mid = rest.astype(bf16).astype(f32)
    terms = jnp.concatenate([high, mid, rest - mid], axis=0).astype(bf16)
    out = dot(terms, w)
    return out[:rows] + out[rows : 2 * rows] + out[2 * rows :]


def kernel(
    cfg,
    obs_hbm,
    act_ref,
    len_ref,
    boot_ref,
    project_hbm,
    out_hbm,
    actw_hbm,
    gain_ref,
    head_ref,
    q_ref,
    grad_ref,
    actgrad_ref,
    rows_all,
    weights,
    out_weight,
    act_weight,
    act_slots,
    keys,
    values,
    embedded,
    last_f32,
    last_bf,
    hid_slots,
    fact_a_src,
    fact_a,
    fact_b_src,
    fact_b,
    extra_src,
    extra,
    partial,
    sib_part,
    row_sum,
    row_parts,
    act_pick,
    act_sum,
    local_sem,
    send_sem,
    recv_sem,
):
    ny, nt, seqs, steps, feats, inner, act_len = cfg
    nz = HALVES * nt
    nyk = ny * CORES
    heads = inner // HEAD_DIM
    rows = seqs * heads
    width = nt * feats
    hist = HALVES * nyk * steps
    half = nyk * steps
    scale = HEAD_DIM ** (-0.5)

    critic = lax.axis_index("critic")
    group = lax.axis_index("tensor")
    y = lax.div(critic, HALVES * CORES)
    zh = lax.rem(lax.div(critic, CORES), HALVES)
    core = lax.rem(critic, CORES)
    z = zh * nt + group
    yk = y * CORES + core

    def dev(y_at, z_at, core_at):
        return {
            "critic": (y_at * HALVES + lax.div(z_at, nt)) * CORES + core_at,
            "tensor": lax.rem(z_at, nt),
        }

    def dev_z(z_at):
        return dev(y, z_at, core)

    def dev_yk(yk_at):
        return dev(lax.div(yk_at, CORES), z, lax.rem(yk_at, CORES))

    sibling = dev(y, z, CORES - 1 - core)

    loads = [
        pltpu.make_async_copy(src, dst, local_sem.at[i])
        for i, (src, dst) in enumerate(
            [
                (obs_hbm, rows_all.at[:, group, zh, y, core]),
                (actw_hbm, act_weight),
                (project_hbm.at[1], weights.at[1]),
                (project_hbm.at[2], weights.at[2]),
                (project_hbm.at[0], weights.at[0]),
                (out_hbm, out_weight),
            ]
        )
    ]
    for load in loads:
        load.start()

    barrier = pltpu.get_barrier_semaphore()
    for d in range(1, nz):
        pl.semaphore_signal(
            barrier, inc=1, device_id=dev_z(mod(z + d, nz)), device_id_type=pl.DeviceIdType.MESH
        )
    for d in range(1, nyk):
        pl.semaphore_signal(
            barrier, inc=1, device_id=dev_yk(mod(yk + d, nyk)), device_id_type=pl.DeviceIdType.MESH
        )

    act_slots[zh, yk] = act_ref[...]

    sends = []
    sem_at = [0]

    def copy_of(src, dst, target, sem):
        return pltpu.make_async_remote_copy(
            src_ref=src,
            dst_ref=dst,
            send_sem=send_sem.at[sem],
            recv_sem=recv_sem.at[sem],
            device_id=target,
            device_id_type=pl.DeviceIdType.MESH,
        )

    def push(src, dst, target):
        sem = sem_at[0]
        sem_at[0] += 1
        copy = copy_of(src, dst, target, sem)
        copy.start()
        sends.append(copy)
        return sem

    def arrive(dst, sem):
        copy_of(dst, dst, sibling, sem).wait_recv()

    def ring(at, count, block, target, forward, backward):
        sems = {}

        def send(step):
            if step < forward:
                ref = block(mod(at - step, count))
                sems[step, 1] = push(ref, ref, target(mod(at + 1, count)))
            if step < backward:
                ref = block(mod(at + step, count))
                sems[step, -1] = push(ref, ref, target(mod(at - 1, count)))

        def recv(step):
            got = []
            if step < forward:
                owner = mod(at - 1 - step, count)
                arrive(block(owner), sems[step, 1])
                got.append(owner)
            if step < backward:
                owner = mod(at + 1 + step, count)
                arrive(block(owner), sems[step, -1])
                got.append(owner)
            return got

        return send, recv, max(forward, backward)

    first = seqs // 2
    near = pl.ds(0, first)
    far = pl.ds(first, seqs - first)

    def near_z(z_at):
        return rows_all.at[near, lax.rem(z_at, nt), lax.div(z_at, nt), y, core]

    def near_y(y_at):
        return rows_all.at[near, :, :, y_at, core]

    def far_y(y_at):
        return rows_all.at[far, group, zh, y_at, core]

    def far_z(z_at):
        return rows_all.at[far, lax.rem(z_at, nt), lax.div(z_at, nt), :, core]

    def dev_y(y_at):
        return dev(y_at, z, core)

    pz_send, pz_recv, pz_steps = ring(z, nz, near_z, dev_z, nz // 2, (nz - 1) // 2)
    py_send, py_recv, py_steps = ring(y, ny, near_y, dev_y, ny // 2, (ny - 1) // 2)
    qy_send, qy_recv, qy_steps = ring(y, ny, far_y, dev_y, (ny - 1) // 2, ny // 2)
    qz_send, qz_recv, qz_steps = ring(z, nz, far_z, dev_z, (nz - 1) // 2, nz // 2)

    other = CORES - 1 - core

    def share_near(y_at):
        ref = near_y(y_at)
        sem = push(ref, ref, sibling)
        return rows_all.at[near, :, :, y_at, other], sem

    def share_far(z_at):
        ref = far_z(z_at)
        sem = push(ref, ref, sibling)
        return rows_all.at[far, lax.rem(z_at, nt), lax.div(z_at, nt), :, other], sem

    pl.semaphore_wait(barrier, nz - 1 + nyk - 1)
    loads[0].wait()
    act_sem = push(act_slots.at[zh, yk], act_slots.at[zh, yk], dev_z(mod(z + nt, nz)))
    pz_send(0)
    qy_send(0)

    arrive(act_slots.at[1 - zh, yk], act_sem)
    act_sems = []
    for d in range(1, nyk):
        ref = act_slots.at[:, yk]
        act_sems.append(push(ref, ref, dev_yk(mod(yk + d, nyk))))
    qy_recv(0)
    for step in range(1, qy_steps):
        qy_send(step)
    pz_recv(0)
    pz_send(1)
    for step in range(1, qy_steps):
        qy_recv(step)
    shared_far = []
    shared_near = []
    qz_send(0)
    shared_far.append(share_far(z))

    for d in range(1, nyk):
        arrive(act_slots.at[:, mod(yk - d, nyk)], act_sems[d - 1])
    act_part = act_ref.shape[1]
    gathered = jnp.zeros((16, act_weight.shape[0]), f32)
    lane = iota((act_part, act_weight.shape[0]), 1)
    lane_row = iota((act_part, act_weight.shape[0]), 0)
    for zh_at in range(HALVES):
        for yk_at in range(nyk):
            c = (yk_at // CORES * HALVES + zh_at) * CORES + yk_at % CORES
            place = (lane == lane_row + c * act_len) & (lane_row < act_len)
            gathered += dot(act_slots[zh_at, yk_at], place.astype(f32).astype(bf16))

    for step in range(1, pz_steps):
        pz_recv(step)
        if step + 1 < pz_steps:
            pz_send(step + 1)
    py_send(0)
    shared_near.append(share_near(y))
    loads[1].wait()
    embedded[...] = dot(gathered.astype(bf16), act_weight[...])

    part = act_len // nt
    pick_shape = act_pick.shape
    col = iota(pick_shape, 1)
    row = iota(pick_shape, 0)
    to_z = lax.div(col, 128)
    within = lax.rem(col, 128)
    to_yk = lax.div(within, part)
    to_critic = (lax.div(to_yk, CORES) * HALVES + lax.div(to_z, nt)) * CORES + lax.rem(to_yk, CORES)
    source = (to_critic * nt + lax.rem(to_z, nt)) * part + lax.rem(within, part)
    act_pick[...] = ((row == source) & (within < nyk * part)).astype(f32).astype(bf16)

    todo = [("q", s) for s in range(qz_steps)]
    for s in range(py_steps):
        todo.insert(2 * s + 1, ("p", s))
    for kind, step in todo:
        if kind == "q":
            got = qz_recv(step)
            if step + 1 < qz_steps:
                qz_send(step + 1)
            shared_far.extend(share_far(owner) for owner in got)
        else:
            got = py_recv(step)
            if step + 1 < py_steps:
                py_send(step + 1)
            shared_near.extend(share_near(owner) for owner in got)

    def position(index):
        zh_at = lax.div(index, half)
        yk_at = lax.div(lax.rem(index, half), steps)
        c = (lax.div(yk_at, CORES) * HALVES + zh_at) * CORES + lax.rem(yk_at, CORES)
        return c * steps + lax.rem(index, steps)

    loads[2].wait()
    loads[3].wait()
    lane_pos = position(iota((16, hist), 1))
    row_pos = position(iota((hist, 128), 0))

    def project(b):
        last = len_ref[b] - 1
        pick = (lane_pos == last).astype(f32).astype(bf16)
        is_last = row_pos == last
        blocks = [rows_all[b, g].reshape(hist, feats) for g in range(nt)]
        own = jnp.concatenate([dot(pick, block) for block in blocks], axis=1)
        full = own[0:8] + embedded[b : b + 1, :]
        last_f32[b : b + 1, :] = full[0:1]
        full_bf = full.astype(bf16).astype(f32)
        key_sum = jnp.zeros((hist, inner), f32)
        value_sum = jnp.zeros((hist, inner), f32)
        for g in range(nt):
            cut = slice(g * feats, (g + 1) * feats)
            mark = jnp.concatenate([is_last] * (feats // 128), axis=1)
            block = jnp.where(mark, full_bf[0:1, cut], blocks[g].astype(f32)).astype(bf16)
            key_sum += dot(block, weights[1, cut, :])
            value_sum += dot(block, weights[2, cut, :])
        keys[b] = key_sum.astype(bf16)
        values[b] = value_sum.astype(bf16)

    last_f32[...] = jnp.zeros_like(last_f32)
    for dst, sem in shared_near:
        arrive(dst, sem)
    for b in range(first):
        project(b)
    for dst, sem in shared_far:
        arrive(dst, sem)
    for b in range(first, seqs):
        project(b)

    loads[4].wait()
    last_rows = last_f32[...]
    last_bf[...] = jnp.concatenate([last_rows, jnp.zeros_like(last_rows)], axis=0).astype(bf16)
    query = dot(last_bf[...], weights[0])[0:8]
    row_id = iota((rows, inner), 0)
    row_head = lax.rem(row_id, heads) == lax.div(iota((rows, inner), 1), HEAD_DIM)

    def spread(x):
        out = jnp.zeros((rows, inner), f32)
        for b in range(seqs):
            out = jnp.where((lax.div(row_id, heads) == b) & row_head, x[b : b + 1, :], out)
        return out

    def fold(x):
        shape = x.shape
        seq_of = lax.div(iota(shape, 0), heads)
        out_row = iota((8, shape[1]), 0)
        out = jnp.zeros((8, shape[1]), f32)
        for b in range(seqs):
            total = jnp.sum(jnp.where(seq_of == b, x, 0.0), axis=0, keepdims=True)
            out = jnp.where(out_row == b, total, out)
        return out

    def per_seq(shape, make):
        seq_of = lax.div(iota(shape, 0), heads)
        out = jnp.zeros(shape, f32)
        for b in range(seqs):
            out = jnp.where(seq_of == b, make(b), out)
        return out

    query_rows = spread(query)
    scores = per_seq((rows, hist), lambda b: dot_split(query_rows, keys[b], NT_DIMS)) * scale
    seq_row = lax.div(iota((rows, hist), 0), heads)
    pos = position(iota((rows, hist), 1))
    length = jnp.zeros((rows, hist), jnp.int32)
    for b in range(seqs):
        length = jnp.where(seq_row == b, len_ref[b], length)
    scores = jnp.where(pos < length, scores, -1e30)
    weight = jnp.exp(scores - jnp.max(scores, axis=1, keepdims=True))
    weight = jnp.where(pos < length, weight, 0.0)
    attention = weight / jnp.sum(weight, axis=1, keepdims=True)
    attention_round = attention.astype(bf16)
    attended = per_seq((rows, inner), lambda b: dot(attention_round, values[b]))
    attended = fold(jnp.where(row_head, attended, 0.0))
    loads[5].wait()
    attended_bf = jnp.concatenate([attended, jnp.zeros_like(attended)], axis=0).astype(bf16)
    head_part = dot(attended_bf, out_weight[...])
    hid_slots[group, 0:seqs, :] = head_part[0:seqs, : width // 2]
    hid_slots[group, seqs : 2 * seqs, :] = head_part[0:seqs, width // 2 :]
    hid_sems = []
    for d in range(1, nt):
        to = mod(group + d, nt)
        hid_sems.append(push(hid_slots.at[group], hid_slots.at[group], dev_z(zh * nt + to)))

    key_vec = dot_split(query_rows, weights[1], NT_DIMS) * scale
    for z_at in range(nz):
        g = z_at % nt
        h = z_at // nt
        fact_a_src[z_at, :, :feats] = key_vec[:, g * feats : (g + 1) * feats].astype(bf16)
        fact_a_src[z_at, :, feats:] = attention_round[:, h * half : (h + 1) * half]
    fact_a[z] = fact_a_src[z]
    a_sems = []
    for d in range(1, nz):
        to = mod(z + d, nz)
        a_sems.append(push(fact_a_src.at[to], fact_a.at[z], dev_z(to)))

    for d in range(1, nt):
        arrive(hid_slots.at[mod(group - d, nt)], hid_sems[d - 1])
    total = hid_slots[0]
    for g in range(1, nt):
        total = total + hid_slots[g]
    zero_rows = jnp.zeros((8 - seqs, width), f32)
    head_sum = jnp.concatenate([total[0:seqs], total[seqs : 2 * seqs]], axis=1)
    hidden = last_rows + jnp.concatenate([head_sum, zero_rows], axis=0)
    gain_head = gain_ref[...] * head_ref[...]
    inverse = lax.rsqrt(jnp.sum(hidden * hidden, axis=1, keepdims=True) * (1.0 / width) + NORM_EPS)
    normed = hidden * inverse
    q_vals = jnp.sum(gain_head * normed, axis=1, keepdims=True)
    q_lane = iota((8, 128), 1)
    q_row = iota((8, 128), 0)
    q_line = jnp.sum(jnp.where(q_lane == q_row, q_vals, 0.0), axis=0, keepdims=True)
    q_ref[...] = q_line[:, 0:seqs]
    boot = jnp.zeros((8, 1), f32)
    for b in range(seqs):
        boot = jnp.where(iota((8, 1), 0) == b, boot_ref[0, b].astype(f32), boot)
    grad_normed = boot * gain_head
    mean = jnp.sum(grad_normed * normed, axis=1, keepdims=True) * (1.0 / width)
    grad_last = inverse * (grad_normed - normed * mean)

    grad_heads = spread(dot_split(grad_last, out_weight[...], NT_DIMS))
    value_vec = dot_split(grad_heads, weights[2], NT_DIMS)
    grad_attention = per_seq((rows, hist), lambda b: dot_split(grad_heads, values[b], NT_DIMS))
    grad_scores = attention * (
        grad_attention - jnp.sum(attention * grad_attention, axis=1, keepdims=True)
    )
    for z_at in range(nz):
        g = z_at % nt
        h = z_at // nt
        fact_b_src[z_at, :, :feats] = value_vec[:, g * feats : (g + 1) * feats].astype(bf16)
        fact_b_src[z_at, :, feats:] = grad_scores[:, h * half : (h + 1) * half].astype(bf16)
    fact_b[z] = fact_b_src[z]
    b_sems = []
    for d in range(1, nz):
        to = mod(z + d, nz)
        b_sems.append(push(fact_b_src.at[to], fact_b.at[z], dev_z(to)))

    grad_query = per_seq((rows, inner), lambda b: dot_split(grad_scores, keys[b]))
    grad_query = fold(jnp.where(row_head, grad_query, 0.0)) * scale
    from_query = dot_split(grad_query, weights[0], NT_DIMS)
    extra_rows = from_query + jnp.where(group == 0, 1.0, 0.0) * grad_last
    at_last = pos == length - 1
    score_last = jnp.sum(jnp.where(at_last, grad_scores, 0.0), axis=1, keepdims=True)
    weight_last = jnp.sum(
        jnp.where(at_last, attention_round.astype(f32), 0.0), axis=1, keepdims=True
    )
    grad_lastrow = extra_rows + fold(score_last * key_vec + weight_last * value_vec)
    act_terms = dot_split(grad_lastrow, act_weight[...], NT_DIMS)
    act_cols = dot_exact(act_terms, act_pick[...])
    cut = feats // 2
    for z_at in range(nz):
        g = z_at % nt
        extra_src[z_at, 0:seqs, :cut] = extra_rows[0:seqs, g * feats : g * feats + cut]
        extra_src[z_at, seqs : 2 * seqs, :cut] = extra_rows[0:seqs, g * feats + cut : (g + 1) * feats]
        extra_src[z_at, :, cut:] = act_cols[:, z_at * 128 : (z_at + 1) * 128]
    extra[z] = extra_src[z]
    x_sems = []
    for d in range(1, nz):
        to = mod(z + d, nz)
        x_sems.append(push(extra_src.at[to], extra.at[z], dev_z(to)))

    for d in range(1, nz):
        arrive(fact_a.at[mod(z - d, nz)], a_sems[d - 1])
    for d in range(1, nz):
        arrive(fact_b.at[mod(z - d, nz)], b_sems[d - 1])
    factors = nz * rows
    vec_a = fact_a[:, :, :feats].reshape(factors, feats)
    vec_b = fact_b[:, :, :feats].reshape(factors, feats)
    coef_a = fact_b[:, :, feats:].reshape(factors, half).astype(f32)
    coef_b = fact_a[:, :, feats:].reshape(factors, half).astype(f32)
    coefs = jnp.concatenate([coef_a.T, coef_b.T], axis=1)
    vecs = jnp.concatenate([vec_a, vec_b], axis=0)
    seq_col = lax.div(lax.rem(iota(coefs.shape, 1), rows), heads)
    for d in range(1, nz):
        arrive(extra.at[mod(z - d, nz)], x_sems[d - 1])
    extra_sum = extra[0]
    for z_at in range(1, nz):
        extra_sum = extra_sum + extra[z_at]
    act_sum[yk] = extra_sum[:, cut:]
    act_sems = []
    for d in range(1, nyk):
        act_sems.append(push(act_sum.at[yk], act_sum.at[yk], dev_yk(mod(yk + d, nyk))))
    extra_full = jnp.concatenate([extra_sum[0:seqs, :cut], extra_sum[seqs : 2 * seqs, :cut]], axis=1)
    here = position(iota((half, feats), 0) + zh * half)
    for b in range(seqs):
        out = dot(jnp.where(seq_col == b, coefs, 0.0).astype(bf16), vecs)
        out = out + jnp.where(here == len_ref[b] - 1, extra_full[b : b + 1, :], 0.0)
        partial[:, :, b] = out.reshape(ny, CORES, steps, feats)

    sib_sem = push(partial.at[:, other], sib_part, sibling)
    arrive(sib_part, sib_sem)
    row_sum[...] = partial[:, core] + sib_part[...]
    y_sems = []
    for d in range(1, ny):
        to = mod(y + d, ny)
        y_sems.append(push(row_sum.at[to], row_parts.at[d - 1], dev_y(to)))
    for d in range(1, nyk):
        arrive(act_sum.at[mod(yk - d, nyk)], act_sems[d - 1])
    act_total = act_sum[0]
    for yk_at in range(1, nyk):
        act_total = act_total + act_sum[yk_at]
    mine = (iota((128, 128), 0) == iota((128, 128), 1) + yk * part) & (iota((128, 128), 1) < part)
    act_mine = dot_exact(act_total, mine.astype(f32).astype(bf16))
    actgrad_ref[...] = act_mine[0:seqs, 0:part]
    result = row_sum[y]
    for d in range(1, ny):
        arrive(row_parts.at[d - 1], y_sems[d - 1])
        result = result + row_parts[d - 1]
    grad_ref[...] = result
    for copy in sends:
        copy.wait_send()


def solution(mesh):
    nt = mesh.shape["tensor"]
    ny = mesh.shape["critic"] // (HALVES * CORES)
    nz = HALVES * nt
    nyk = ny * CORES

    def on_device(obs, actions, lengths, boot, project, out_weight, act_weight, gain, head):
        seqs, steps, feats = obs.shape
        width, inner = project.shape[1], project.shape[3]
        act_len = actions.shape[1]
        rows = seqs * (inner // HEAD_DIM)
        hist = steps * HALVES * nyk
        half = steps * nyk
        weights = jnp.transpose(project[0], (1, 0, 2))
        padded = jnp.pad(actions, ((0, 16 - seqs), (0, 128 - act_len)))
        vmem = pl.BlockSpec(memory_space=pltpu.VMEM)
        smem = pl.BlockSpec(memory_space=pltpu.SMEM)
        hbm = pl.BlockSpec(memory_space=pl.ANY)
        part = act_len // nt
        flops = 4 * seqs * hist * width * inner
        return pl.pallas_call(
            functools.partial(kernel, (ny, nt, seqs, steps, feats, inner, act_len)),
            out_shape=(
                jax.ShapeDtypeStruct((1, seqs), f32),
                jax.ShapeDtypeStruct((seqs, steps, feats), f32),
                jax.ShapeDtypeStruct((seqs, part), f32),
            ),
            in_specs=[hbm, vmem, smem, smem, hbm, hbm, hbm, vmem, vmem],
            out_specs=(vmem, vmem, vmem),
            scratch_shapes=[
                pltpu.VMEM((seqs, nt, HALVES, ny, CORES, steps, feats), bf16),
                pltpu.VMEM((3, width, inner), bf16),
                pltpu.VMEM((inner, width), bf16),
                pltpu.VMEM(act_weight.shape[1:], bf16),
                pltpu.VMEM((HALVES, nyk, 16, 128), bf16),
                pltpu.VMEM((seqs, hist, inner), bf16),
                pltpu.VMEM((seqs, hist, inner), bf16),
                pltpu.VMEM((16, width), f32),
                pltpu.VMEM((8, width), f32),
                pltpu.VMEM((16, width), bf16),
                pltpu.VMEM((nt, 8, width // 2), f32),
                pltpu.VMEM((nz, rows, feats + half), bf16),
                pltpu.VMEM((nz, rows, feats + half), bf16),
                pltpu.VMEM((nz, rows, feats + half), bf16),
                pltpu.VMEM((nz, rows, feats + half), bf16),
                pltpu.VMEM((nz, 8, feats // 2 + 128), f32),
                pltpu.VMEM((nz, 8, feats // 2 + 128), f32),
                pltpu.VMEM((ny, CORES, seqs, steps, feats), f32),
                pltpu.VMEM((ny, seqs, steps, feats), f32),
                pltpu.VMEM((ny, seqs, steps, feats), f32),
                pltpu.VMEM((ny - 1, seqs, steps, feats), f32),
                pltpu.VMEM((act_weight.shape[1], nz * 128), bf16),
                pltpu.VMEM((nyk, 8, 128), f32),
                pltpu.SemaphoreType.DMA((6,)),
                pltpu.SemaphoreType.DMA((96,)),
                pltpu.SemaphoreType.DMA((96,)),
            ],
            compiler_params=pltpu.CompilerParams(
                collective_id=0, has_side_effects=True, vmem_limit_bytes=48 * 1024 * 1024
            ),
            cost_estimate=pl.CostEstimate(
                flops=flops, bytes_accessed=10 * 1024 * 1024, transcendentals=seqs * hist
            ),
        )(obs, padded, lengths, boot, weights, out_weight[0], act_weight[0], gain, head)

    in_specs = (
        P("seq", "critic", "tensor"),
        P("seq", "critic"),
        P("seq"),
        P("critic", "seq"),
        P("critic", None, None, "tensor"),
        P("critic", "tensor", None),
        P("critic", None, None),
        P("critic", None),
        P("critic", None),
    )
    out_specs = (P("critic", "seq"), P("seq", "critic", "tensor"), P("seq", ("critic", "tensor")))
    return jax.shard_map(
        on_device, mesh=mesh, in_specs=in_specs, out_specs=out_specs, check_vma=False
    )
```

```python
import functools

import jax
import jax.numpy as jnp
from jax import lax
from jax.experimental import pallas as pl
from jax.experimental.pallas import tpu as pltpu
from jax.sharding import PartitionSpec as P

HEAD_DIM = 128
NORM_EPS = 1e-05
CORES = 2
HALVES = 2

f32 = jnp.float32
bf16 = jnp.bfloat16
NN = (((1,), (0,)), ((), ()))
NT_DIMS = (((1,), (1,)), ((), ()))


def mod(value, count):
    return lax.rem(value + count, count)


def iota(shape, axis):
    return lax.broadcasted_iota(jnp.int32, shape, axis)


def split(x):
    high = x.astype(bf16).astype(f32)
    return jnp.concatenate([high, x - high], axis=0).astype(bf16)


def dot(x, w, dims=NN):
    return lax.dot_general(x, w, dims, preferred_element_type=f32)


def dot_split(x, w, dims=NN):
    rows = x.shape[0]
    both = dot(split(x), w, dims)
    return both[:rows] + both[rows:]


def dot_exact(x, w):
    rows = x.shape[0]
    high = x.astype(bf16).astype(f32)
    rest = x - high
    mid = rest.astype(bf16).astype(f32)
    terms = jnp.concatenate([high, mid, rest - mid], axis=0).astype(bf16)
    out = dot(terms, w)
    return out[:rows] + out[rows : 2 * rows] + out[2 * rows :]


def kernel(
    cfg,
    obs_hbm,
    act_hbm,
    len_hbm,
    boot_hbm,
    project_hbm,
    out_hbm,
    actw_hbm,
    gain_hbm,
    head_hbm,
    q_ref,
    grad_ref,
    actgrad_ref,
    rows_all,
    weights,
    out_weight,
    act_weight,
    act_slots,
    keys,
    values,
    embedded,
    last_f32,
    last_bf,
    hid_slots,
    fact_a_src,
    fact_a,
    fact_b_src,
    fact_b,
    extra_src,
    extra,
    partial,
    sib_part,
    row_sum,
    row_parts,
    act_pick,
    act_sum,
    len_ref,
    boot_ref,
    gain_ref,
    head_ref,
    local_sem,
    send_sem,
    recv_sem,
):
    ny, nt, seqs, steps, feats, inner, act_len = cfg
    nz = HALVES * nt
    nyk = ny * CORES
    heads = inner // HEAD_DIM
    rows = seqs * heads
    width = nt * feats
    hist = HALVES * nyk * steps
    half = nyk * steps
    scale = HEAD_DIM ** (-0.5)

    critic = lax.axis_index("critic")
    group = lax.axis_index("tensor")
    y = lax.div(critic, HALVES * CORES)
    zh = lax.rem(lax.div(critic, CORES), HALVES)
    core = lax.rem(critic, CORES)
    z = zh * nt + group
    yk = y * CORES + core

    def dev(y_at, z_at, core_at):
        return {
            "critic": (y_at * HALVES + lax.div(z_at, nt)) * CORES + core_at,
            "tensor": lax.rem(z_at, nt),
        }

    def dev_z(z_at):
        return dev(y, z_at, core)

    def dev_yk(yk_at):
        return dev(lax.div(yk_at, CORES), z, lax.rem(yk_at, CORES))

    sibling = dev(y, z, CORES - 1 - core)

    loads = [
        pltpu.make_async_copy(src, dst, local_sem.at[i])
        for i, (src, dst) in enumerate(
            [
                (obs_hbm, rows_all.at[:, group, zh, y, core]),
                (actw_hbm, act_weight),
                (project_hbm.at[1], weights.at[1]),
                (project_hbm.at[2], weights.at[2]),
                (project_hbm.at[0], weights.at[0]),
                (out_hbm, out_weight),
                (act_hbm, act_slots.at[zh, yk]),
                (len_hbm, len_ref),
                (boot_hbm, boot_ref),
                (gain_hbm, gain_ref),
                (head_hbm, head_ref),
            ]
        )
    ]
    for load in loads:
        load.start()

    barrier = pltpu.get_barrier_semaphore()
    for d in range(1, nz):
        pl.semaphore_signal(
            barrier, inc=1, device_id=dev_z(mod(z + d, nz)), device_id_type=pl.DeviceIdType.MESH
        )
    for d in range(1, nyk):
        pl.semaphore_signal(
            barrier, inc=1, device_id=dev_yk(mod(yk + d, nyk)), device_id_type=pl.DeviceIdType.MESH
        )

    part = act_len // nt
    pick_shape = act_pick.shape
    col = iota(pick_shape, 1)
    row = iota(pick_shape, 0)
    to_z = lax.div(col, 128)
    within = lax.rem(col, 128)
    to_yk = lax.div(within, part)
    to_critic = (lax.div(to_yk, CORES) * HALVES + lax.div(to_z, nt)) * CORES + lax.rem(to_yk, CORES)
    source = (to_critic * nt + lax.rem(to_z, nt)) * part + lax.rem(within, part)
    act_pick[...] = ((row == source) & (within < nyk * part)).astype(f32).astype(bf16)

    sends = []
    sem_at = [0]

    def copy_of(src, dst, target, sem):
        return pltpu.make_async_remote_copy(
            src_ref=src,
            dst_ref=dst,
            send_sem=send_sem.at[sem],
            recv_sem=recv_sem.at[sem],
            device_id=target,
            device_id_type=pl.DeviceIdType.MESH,
        )

    def push(src, dst, target):
        sem = sem_at[0]
        sem_at[0] += 1
        copy = copy_of(src, dst, target, sem)
        copy.start()
        sends.append(copy)
        return sem

    def arrive(dst, sem):
        copy_of(dst, dst, sibling, sem).wait_recv()

    def ring(at, count, block, target, forward, backward):
        sems = {}

        def send(step):
            if step < forward:
                ref = block(mod(at - step, count))
                sems[step, 1] = push(ref, ref, target(mod(at + 1, count)))
            if step < backward:
                ref = block(mod(at + step, count))
                sems[step, -1] = push(ref, ref, target(mod(at - 1, count)))

        def recv(step):
            got = []
            if step < forward:
                owner = mod(at - 1 - step, count)
                arrive(block(owner), sems[step, 1])
                got.append(owner)
            if step < backward:
                owner = mod(at + 1 + step, count)
                arrive(block(owner), sems[step, -1])
                got.append(owner)
            return got

        return send, recv, max(forward, backward)

    first = seqs // 2
    near = pl.ds(0, first)
    far = pl.ds(first, seqs - first)
    other = CORES - 1 - core

    def block_at(part, z_at, y_at):
        return rows_all.at[part, lax.rem(z_at, nt), lax.div(z_at, nt), y_at, core]

    def dev_y(y_at):
        return dev(y_at, z, core)

    def share(part, z_at):
        ref = rows_all.at[part, lax.rem(z_at, nt), lax.div(z_at, nt), :, core]
        sem = push(ref, ref, sibling)
        return rows_all.at[part, lax.rem(z_at, nt), lax.div(z_at, nt), :, other], sem

    shared_near = []
    shared_far = []
    act_sems = []
    steps_up = nz // 2
    steps_down = (nz - 1) // 2
    near_ring = ring(z, nz, lambda z_at: block_at(near, z_at, y), dev_z, steps_up, steps_down)
    far_rings = []
    for d in range(ny):
        y_at = mod(y - d, ny)
        ups, downs = (steps_up, steps_down) if d % 2 else (steps_down, steps_up)
        far_rings.append(
            ring(z, nz, functools.partial(lambda y_at, z_at: block_at(far, z_at, y_at), y_at), dev_z, ups, downs)
        )
    ring_steps = max(steps_up, steps_down)

    def spread_y(z_at):
        ref = block_at(near, z_at, y)
        return z_at, [push(ref, ref, dev_y(mod(y + d, ny))) for d in range(1, ny)]

    def finish_near(owner, sems):
        for d, sem in zip(range(1, ny), sems):
            arrive(block_at(near, owner, mod(y - d, ny)), sem)
        shared_near.append(share(near, owner))

    def prepare_actions():
        for d in range(1, nyk):
            arrive(act_slots.at[:, mod(yk - d, nyk)], act_sems[d - 1])
        act_part = act_slots.shape[3]
        gathered = jnp.zeros((16, act_weight.shape[0]), f32)
        lane = iota((act_part, act_weight.shape[0]), 1)
        lane_row = iota((act_part, act_weight.shape[0]), 0)
        for zh_at in range(HALVES):
            for yk_at in range(nyk):
                c = (yk_at // CORES * HALVES + zh_at) * CORES + yk_at % CORES
                place = (lane == lane_row + c * act_len) & (lane_row < act_len)
                gathered += dot(act_slots[zh_at, yk_at], place.astype(f32).astype(bf16))

        loads[1].wait()
        embedded[...] = dot(gathered.astype(bf16), act_weight[...])

    pl.semaphore_wait(barrier, nz - 1 + nyk - 1)
    loads[0].wait()
    near_send, near_recv, _ = near_ring
    near_send(0)
    far_rings[0][0](0)
    far_y = []
    for d in range(1, ny):
        ref = block_at(far, z, y)
        far_y.append(push(ref, ref, dev_y(mod(y + d, ny))))
    waiting = [spread_y(z)]
    loads[6].wait()
    act_sem = push(act_slots.at[zh, yk], act_slots.at[zh, yk], dev_z(mod(z + nt, nz)))
    for d in range(1, ny):
        arrive(block_at(far, z, mod(y - d, ny)), far_y[d - 1])
        far_rings[d][0](0)
    shared_far.append(share(far, z))
    for step in range(ring_steps):
        got = near_recv(step)
        if step + 1 < ring_steps:
            near_send(step + 1)
        came = [spread_y(owner) for owner in got]
        far_got = []
        for send, recv, _ in far_rings:
            owners = recv(step)
            if step + 1 < ring_steps:
                send(step + 1)
            far_got = owners if len(owners) > len(far_got) else far_got
        if step + 1 < ring_steps:
            shared_far.extend(share(far, owner) for owner in far_got)
        for item in waiting:
            finish_near(*item)
        waiting = came
        if step == 0:
            arrive(act_slots.at[1 - zh, yk], act_sem)
            for d in range(1, nyk):
                ref = act_slots.at[:, yk]
                act_sems.append(push(ref, ref, dev_yk(mod(yk + d, nyk))))
        if step == 2:
            prepare_actions()
    for item in waiting:
        finish_near(*item)
    if steps_up == steps_down:
        shared_far.extend(share(far, owner) for owner in far_got)
    else:
        shared_far.append(share(far, mod(z + ring_steps, nz)))

    def position(index):
        zh_at = lax.div(index, half)
        yk_at = lax.div(lax.rem(index, half), steps)
        c = (lax.div(yk_at, CORES) * HALVES + zh_at) * CORES + lax.rem(yk_at, CORES)
        return c * steps + lax.rem(index, steps)

    for load in loads[2:4] + loads[7:]:
        load.wait()
    lane_pos = position(iota((16, hist), 1))
    row_pos = position(iota((hist, 128), 0))

    def project(b):
        last = len_ref[b] - 1
        pick = (lane_pos == last).astype(f32).astype(bf16)
        is_last = row_pos == last
        blocks = [rows_all[b, g].reshape(hist, feats) for g in range(nt)]
        own = jnp.concatenate([dot(pick, block) for block in blocks], axis=1)
        full = own[0:8] + embedded[b : b + 1, :]
        last_f32[b : b + 1, :] = full[0:1]
        full_bf = full.astype(bf16).astype(f32)
        key_sum = jnp.zeros((hist, inner), f32)
        value_sum = jnp.zeros((hist, inner), f32)
        for g in range(nt):
            cut = slice(g * feats, (g + 1) * feats)
            mark = jnp.concatenate([is_last] * (feats // 128), axis=1)
            block = jnp.where(mark, full_bf[0:1, cut], blocks[g].astype(f32)).astype(bf16)
            key_sum += dot(block, weights[1, cut, :])
            value_sum += dot(block, weights[2, cut, :])
        keys[b] = key_sum.astype(bf16)
        values[b] = value_sum.astype(bf16)

    last_f32[...] = jnp.zeros_like(last_f32)
    for dst, sem in shared_near:
        arrive(dst, sem)
    for b in range(first):
        project(b)
    for dst, sem in shared_far:
        arrive(dst, sem)
    for b in range(first, seqs):
        project(b)

    loads[4].wait()
    last_rows = last_f32[...]
    last_bf[...] = jnp.concatenate([last_rows, jnp.zeros_like(last_rows)], axis=0).astype(bf16)
    query = dot(last_bf[...], weights[0])[0:8]
    row_id = iota((rows, inner), 0)
    row_head = lax.rem(row_id, heads) == lax.div(iota((rows, inner), 1), HEAD_DIM)

    def spread(x):
        out = jnp.zeros((rows, inner), f32)
        for b in range(seqs):
            out = jnp.where((lax.div(row_id, heads) == b) & row_head, x[b : b + 1, :], out)
        return out

    def fold(x):
        shape = x.shape
        seq_of = lax.div(iota(shape, 0), heads)
        out_row = iota((8, shape[1]), 0)
        out = jnp.zeros((8, shape[1]), f32)
        for b in range(seqs):
            total = jnp.sum(jnp.where(seq_of == b, x, 0.0), axis=0, keepdims=True)
            out = jnp.where(out_row == b, total, out)
        return out

    def per_seq(shape, make):
        seq_of = lax.div(iota(shape, 0), heads)
        out = jnp.zeros(shape, f32)
        for b in range(seqs):
            out = jnp.where(seq_of == b, make(b), out)
        return out

    query_rows = spread(query)
    scores = per_seq((rows, hist), lambda b: dot_split(query_rows, keys[b], NT_DIMS)) * scale
    seq_row = lax.div(iota((rows, hist), 0), heads)
    pos = position(iota((rows, hist), 1))
    length = jnp.zeros((rows, hist), jnp.int32)
    for b in range(seqs):
        length = jnp.where(seq_row == b, len_ref[b], length)
    scores = jnp.where(pos < length, scores, -1e30)
    weight = jnp.exp(scores - jnp.max(scores, axis=1, keepdims=True))
    weight = jnp.where(pos < length, weight, 0.0)
    attention = weight / jnp.sum(weight, axis=1, keepdims=True)
    attention_round = attention.astype(bf16)
    attended = per_seq((rows, inner), lambda b: dot(attention_round, values[b]))
    attended = fold(jnp.where(row_head, attended, 0.0))
    loads[5].wait()
    attended_bf = jnp.concatenate([attended, jnp.zeros_like(attended)], axis=0).astype(bf16)
    head_part = dot(attended_bf, out_weight[...])
    hid_slots[group, 0:seqs, :] = head_part[0:seqs, : width // 2]
    hid_slots[group, seqs : 2 * seqs, :] = head_part[0:seqs, width // 2 :]
    hid_sems = []
    for d in range(1, nt):
        to = mod(group + d, nt)
        hid_sems.append(push(hid_slots.at[group], hid_slots.at[group], dev_z(zh * nt + to)))

    key_vec = dot_split(query_rows, weights[1], NT_DIMS) * scale
    for z_at in range(nz):
        g = z_at % nt
        h = z_at // nt
        fact_a_src[z_at, :, :feats] = key_vec[:, g * feats : (g + 1) * feats].astype(bf16)
        fact_a_src[z_at, :, feats:] = attention_round[:, h * half : (h + 1) * half]
    fact_a[z] = fact_a_src[z]
    a_sems = []
    for d in range(1, nz):
        to = mod(z + d, nz)
        a_sems.append(push(fact_a_src.at[to], fact_a.at[z], dev_z(to)))

    for d in range(1, nt):
        arrive(hid_slots.at[mod(group - d, nt)], hid_sems[d - 1])
    total = hid_slots[0]
    for g in range(1, nt):
        total = total + hid_slots[g]
    zero_rows = jnp.zeros((8 - seqs, width), f32)
    head_sum = jnp.concatenate([total[0:seqs], total[seqs : 2 * seqs]], axis=1)
    hidden = last_rows + jnp.concatenate([head_sum, zero_rows], axis=0)
    gain_head = gain_ref[...] * head_ref[...]
    inverse = lax.rsqrt(jnp.sum(hidden * hidden, axis=1, keepdims=True) * (1.0 / width) + NORM_EPS)
    normed = hidden * inverse
    q_vals = jnp.sum(gain_head * normed, axis=1, keepdims=True)
    q_lane = iota((8, 128), 1)
    q_row = iota((8, 128), 0)
    q_line = jnp.sum(jnp.where(q_lane == q_row, q_vals, 0.0), axis=0, keepdims=True)
    q_ref[...] = q_line[:, 0:seqs]
    boot = jnp.zeros((8, 1), f32)
    for b in range(seqs):
        boot = jnp.where(iota((8, 1), 0) == b, boot_ref[0, b].astype(f32), boot)
    grad_normed = boot * gain_head
    mean = jnp.sum(grad_normed * normed, axis=1, keepdims=True) * (1.0 / width)
    grad_last = inverse * (grad_normed - normed * mean)

    grad_heads = spread(dot_split(grad_last, out_weight[...], NT_DIMS))
    value_vec = dot_split(grad_heads, weights[2], NT_DIMS)
    grad_attention = per_seq((rows, hist), lambda b: dot_split(grad_heads, values[b], NT_DIMS))
    grad_scores = attention * (
        grad_attention - jnp.sum(attention * grad_attention, axis=1, keepdims=True)
    )
    for z_at in range(nz):
        g = z_at % nt
        h = z_at // nt
        fact_b_src[z_at, :, :feats] = value_vec[:, g * feats : (g + 1) * feats].astype(bf16)
        fact_b_src[z_at, :, feats:] = grad_scores[:, h * half : (h + 1) * half].astype(bf16)
    fact_b[z] = fact_b_src[z]
    b_sems = []
    for d in range(1, nz):
        to = mod(z + d, nz)
        b_sems.append(push(fact_b_src.at[to], fact_b.at[z], dev_z(to)))

    grad_query = per_seq((rows, inner), lambda b: dot_split(grad_scores, keys[b]))
    grad_query = fold(jnp.where(row_head, grad_query, 0.0)) * scale
    from_query = dot_split(grad_query, weights[0], NT_DIMS)
    extra_rows = from_query + jnp.where(group == 0, 1.0, 0.0) * grad_last
    at_last = pos == length - 1
    score_last = jnp.sum(jnp.where(at_last, grad_scores, 0.0), axis=1, keepdims=True)
    weight_last = jnp.sum(
        jnp.where(at_last, attention_round.astype(f32), 0.0), axis=1, keepdims=True
    )
    grad_lastrow = extra_rows + fold(score_last * key_vec + weight_last * value_vec)
    act_terms = dot_split(grad_lastrow, act_weight[...], NT_DIMS)
    act_cols = dot_exact(act_terms, act_pick[...])
    cut = feats // 2
    for z_at in range(nz):
        g = z_at % nt
        extra_src[z_at, 0:seqs, :cut] = extra_rows[0:seqs, g * feats : g * feats + cut]
        extra_src[z_at, seqs : 2 * seqs, :cut] = extra_rows[0:seqs, g * feats + cut : (g + 1) * feats]
        extra_src[z_at, :, cut:] = act_cols[:, z_at * 128 : (z_at + 1) * 128]
    extra[z] = extra_src[z]
    x_sems = []
    for d in range(1, nz):
        to = mod(z + d, nz)
        x_sems.append(push(extra_src.at[to], extra.at[z], dev_z(to)))

    for d in range(1, nz):
        arrive(fact_a.at[mod(z - d, nz)], a_sems[d - 1])
    for d in range(1, nz):
        arrive(fact_b.at[mod(z - d, nz)], b_sems[d - 1])
    factors = nz * rows
    vec_a = fact_a[:, :, :feats].reshape(factors, feats)
    vec_b = fact_b[:, :, :feats].reshape(factors, feats)
    coef_a = fact_b[:, :, feats:].reshape(factors, half).astype(f32)
    coef_b = fact_a[:, :, feats:].reshape(factors, half).astype(f32)
    coefs = jnp.concatenate([coef_a.T, coef_b.T], axis=1)
    vecs = jnp.concatenate([vec_a, vec_b], axis=0)
    seq_col = lax.div(lax.rem(iota(coefs.shape, 1), rows), heads)
    for d in range(1, nz):
        arrive(extra.at[mod(z - d, nz)], x_sems[d - 1])
    extra_sum = extra[0]
    for z_at in range(1, nz):
        extra_sum = extra_sum + extra[z_at]
    act_sum[yk] = extra_sum[:, cut:]
    act_sems = []
    for d in range(1, nyk):
        act_sems.append(push(act_sum.at[yk], act_sum.at[yk], dev_yk(mod(yk + d, nyk))))
    extra_full = jnp.concatenate([extra_sum[0:seqs, :cut], extra_sum[seqs : 2 * seqs, :cut]], axis=1)
    here = position(iota((half, feats), 0) + zh * half)
    for b in range(seqs):
        out = dot(jnp.where(seq_col == b, coefs, 0.0).astype(bf16), vecs)
        out = out + jnp.where(here == len_ref[b] - 1, extra_full[b : b + 1, :], 0.0)
        partial[:, :, b] = out.reshape(ny, CORES, steps, feats)

    sib_sem = push(partial.at[:, other], sib_part, sibling)
    arrive(sib_part, sib_sem)
    row_sum[...] = partial[:, core] + sib_part[...]
    y_sems = []
    for d in range(1, ny):
        to = mod(y + d, ny)
        y_sems.append(push(row_sum.at[to], row_parts.at[d - 1], dev_y(to)))
    for d in range(1, nyk):
        arrive(act_sum.at[mod(yk - d, nyk)], act_sems[d - 1])
    act_total = act_sum[0]
    for yk_at in range(1, nyk):
        act_total = act_total + act_sum[yk_at]
    mine = (iota((128, 128), 0) == iota((128, 128), 1) + yk * part) & (iota((128, 128), 1) < part)
    act_mine = dot_exact(act_total, mine.astype(f32).astype(bf16))
    actgrad_ref[...] = act_mine[0:seqs, 0:part]
    result = row_sum[y]
    for d in range(1, ny):
        arrive(row_parts.at[d - 1], y_sems[d - 1])
        result = result + row_parts[d - 1]
    grad_ref[...] = result
    for copy in sends:
        copy.wait_send()


def solution(mesh):
    nt = mesh.shape["tensor"]
    ny = mesh.shape["critic"] // (HALVES * CORES)
    nz = HALVES * nt
    nyk = ny * CORES

    def on_device(obs, actions, lengths, boot, project, out_weight, act_weight, gain, head):
        seqs, steps, feats = obs.shape
        width, inner = project.shape[1], project.shape[3]
        act_len = actions.shape[1]
        rows = seqs * (inner // HEAD_DIM)
        hist = steps * HALVES * nyk
        half = steps * nyk
        weights = jnp.transpose(project[0], (1, 0, 2))
        padded = jnp.pad(actions, ((0, 16 - seqs), (0, 128 - act_len)))
        vmem = pl.BlockSpec(memory_space=pltpu.VMEM)
        hbm = pl.BlockSpec(memory_space=pltpu.HBM)
        part = act_len // nt
        flops = 4 * seqs * hist * width * inner
        return pl.pallas_call(
            functools.partial(kernel, (ny, nt, seqs, steps, feats, inner, act_len)),
            out_shape=(
                jax.ShapeDtypeStruct((1, seqs), f32),
                jax.ShapeDtypeStruct((seqs, steps, feats), f32),
                jax.ShapeDtypeStruct((seqs, part), f32),
            ),
            in_specs=[hbm] * 9,
            out_specs=(vmem, vmem, vmem),
            scratch_shapes=[
                pltpu.VMEM((seqs, nt, HALVES, ny, CORES, steps, feats), bf16),
                pltpu.VMEM((3, width, inner), bf16),
                pltpu.VMEM((inner, width), bf16),
                pltpu.VMEM(act_weight.shape[1:], bf16),
                pltpu.VMEM((HALVES, nyk, 16, 128), bf16),
                pltpu.VMEM((seqs, hist, inner), bf16),
                pltpu.VMEM((seqs, hist, inner), bf16),
                pltpu.VMEM((16, width), f32),
                pltpu.VMEM((8, width), f32),
                pltpu.VMEM((16, width), bf16),
                pltpu.VMEM((nt, 8, width // 2), f32),
                pltpu.VMEM((nz, rows, feats + half), bf16),
                pltpu.VMEM((nz, rows, feats + half), bf16),
                pltpu.VMEM((nz, rows, feats + half), bf16),
                pltpu.VMEM((nz, rows, feats + half), bf16),
                pltpu.VMEM((nz, 8, feats // 2 + 128), f32),
                pltpu.VMEM((nz, 8, feats // 2 + 128), f32),
                pltpu.VMEM((ny, CORES, seqs, steps, feats), f32),
                pltpu.VMEM((ny, seqs, steps, feats), f32),
                pltpu.VMEM((ny, seqs, steps, feats), f32),
                pltpu.VMEM((ny - 1, seqs, steps, feats), f32),
                pltpu.VMEM((act_weight.shape[1], nz * 128), bf16),
                pltpu.VMEM((nyk, 8, 128), f32),
                pltpu.SMEM((seqs,), jnp.int32),
                pltpu.SMEM((1, seqs), jnp.int32),
                pltpu.VMEM((1, width), f32),
                pltpu.VMEM((1, width), f32),
                pltpu.SemaphoreType.DMA((11,)),
                pltpu.SemaphoreType.DMA((160,)),
                pltpu.SemaphoreType.DMA((160,)),
            ],
            compiler_params=pltpu.CompilerParams(
                collective_id=0, has_side_effects=True, vmem_limit_bytes=63 * 1024 * 1024
            ),
            cost_estimate=pl.CostEstimate(
                flops=flops, bytes_accessed=10 * 1024 * 1024, transcendentals=seqs * hist
            ),
        )(obs, padded, lengths, boot, weights, out_weight[0], act_weight[0], gain, head)

    in_specs = (
        P("seq", "critic", "tensor"),
        P("seq", "critic"),
        P("seq"),
        P("critic", "seq"),
        P("critic", None, None, "tensor"),
        P("critic", "tensor", None),
        P("critic", None, None),
        P("critic", None),
        P("critic", None),
    )
    out_specs = (P("critic", "seq"), P("seq", "critic", "tensor"), P("seq", ("critic", "tensor")))
    return jax.shard_map(
        on_device, mesh=mesh, in_specs=in_specs, out_specs=out_specs, check_vma=False
    )
```

```python
import functools

import jax
import jax.numpy as jnp
from jax import lax
from jax.experimental import pallas as pl
from jax.experimental.pallas import tpu as pltpu
from jax.sharding import PartitionSpec as P

HEAD_DIM = 128
NORM_EPS = 1e-05
CORES = 2
HALVES = 2

f32 = jnp.float32
bf16 = jnp.bfloat16
NN = (((1,), (0,)), ((), ()))
NT_DIMS = (((1,), (1,)), ((), ()))


def mod(value, count):
    return lax.rem(value + count, count)


def iota(shape, axis):
    return lax.broadcasted_iota(jnp.int32, shape, axis)


def split(x):
    high = x.astype(bf16).astype(f32)
    return jnp.concatenate([high, x - high], axis=0).astype(bf16)


def dot(x, w, dims=NN):
    return lax.dot_general(x, w, dims, preferred_element_type=f32)


def dot_split(x, w, dims=NN):
    rows = x.shape[0]
    both = dot(split(x), w, dims)
    return both[:rows] + both[rows:]


def dot_exact(x, w):
    rows = x.shape[0]
    high = x.astype(bf16).astype(f32)
    rest = x - high
    mid = rest.astype(bf16).astype(f32)
    terms = jnp.concatenate([high, mid, rest - mid], axis=0).astype(bf16)
    out = dot(terms, w)
    return out[:rows] + out[rows : 2 * rows] + out[2 * rows :]


def kernel(
    cfg,
    obs_hbm,
    act_hbm,
    len_hbm,
    boot_hbm,
    project_hbm,
    out_hbm,
    actw_hbm,
    gain_hbm,
    head_hbm,
    out_ref,
    rows_all,
    weights,
    out_weight,
    act_weight,
    act_slots,
    keys,
    values,
    embedded,
    last_f32,
    last_bf,
    hid_slots,
    fact_a_src,
    fact_a,
    fact_c_src,
    fact_c,
    fact_b_src,
    fact_b,
    extra_src,
    extra,
    partial,
    sib_part,
    row_sum,
    row_send,
    row_parts,
    act_pick,
    act_sum,
    act_raw,
    act_pad,
    len_ref,
    boot_ref,
    gain_ref,
    head_ref,
    local_sem,
    send_sem,
    recv_sem,
):
    ny, nt, seqs, steps, feats, inner, act_len = cfg
    nz = HALVES * nt
    nyk = ny * CORES
    heads = inner // HEAD_DIM
    rows = seqs * heads
    width = nt * feats
    hist = HALVES * nyk * steps
    half = nyk * steps
    scale = HEAD_DIM ** (-0.5)

    critic = lax.axis_index("critic")
    group = lax.axis_index("tensor")
    y = lax.div(critic, HALVES * CORES)
    zh = lax.rem(lax.div(critic, CORES), HALVES)
    core = lax.rem(critic, CORES)
    z = zh * nt + group
    yk = y * CORES + core

    def dev(y_at, z_at, core_at):
        return {
            "critic": (y_at * HALVES + lax.div(z_at, nt)) * CORES + core_at,
            "tensor": lax.rem(z_at, nt),
        }

    def dev_z(z_at):
        return dev(y, z_at, core)

    def dev_yk(yk_at):
        return dev(lax.div(yk_at, CORES), z, lax.rem(yk_at, CORES))

    sibling = dev(y, z, CORES - 1 - core)

    far_first = sorted(range(1, nz), key=lambda d: -min(d, nz - d))

    loads = [
        pltpu.make_async_copy(src, dst, local_sem.at[i])
        for i, (src, dst) in enumerate(
            [
                (obs_hbm, rows_all.at[:, group, zh, y, core]),
                (actw_hbm, act_weight),
                (project_hbm.at[1], weights.at[1]),
                (project_hbm.at[2], weights.at[2]),
                (project_hbm.at[0], weights.at[0]),
                (out_hbm, out_weight),
                (act_hbm, act_raw),
                (len_hbm, len_ref),
                (boot_hbm, boot_ref),
                (gain_hbm, gain_ref),
                (head_hbm, head_ref),
            ]
        )
    ]
    for load in loads:
        load.start()

    barrier = pltpu.get_barrier_semaphore()
    for d in range(1, nz):
        pl.semaphore_signal(
            barrier, inc=1, device_id=dev_z(mod(z + d, nz)), device_id_type=pl.DeviceIdType.MESH
        )
    for d in range(1, nyk):
        pl.semaphore_signal(
            barrier, inc=1, device_id=dev_yk(mod(yk + d, nyk)), device_id_type=pl.DeviceIdType.MESH
        )

    part = act_len // nt
    pick_shape = act_pick.shape
    col = iota(pick_shape, 1)
    row = iota(pick_shape, 0)
    to_z = lax.div(col, 128)
    within = lax.rem(col, 128)
    to_yk = lax.div(within, part)
    to_critic = (lax.div(to_yk, CORES) * HALVES + lax.div(to_z, nt)) * CORES + lax.rem(to_yk, CORES)
    source = (to_critic * nt + lax.rem(to_z, nt)) * part + lax.rem(within, part)
    act_pick[...] = ((row == source) & (within < nyk * part)).astype(f32).astype(bf16)

    sends = []
    sem_at = [0]

    def copy_of(src, dst, target, sem):
        return pltpu.make_async_remote_copy(
            src_ref=src,
            dst_ref=dst,
            send_sem=send_sem.at[sem],
            recv_sem=recv_sem.at[sem],
            device_id=target,
            device_id_type=pl.DeviceIdType.MESH,
        )

    def push(src, dst, target):
        sem = sem_at[0]
        sem_at[0] += 1
        copy = copy_of(src, dst, target, sem)
        copy.start()
        sends.append(copy)
        return sem

    def arrive(dst, sem):
        copy_of(dst, dst, sibling, sem).wait_recv()

    def ring(at, count, block, target, forward, backward):
        sems = {}

        def send(step):
            if step < forward:
                ref = block(mod(at - step, count))
                sems[step, 1] = push(ref, ref, target(mod(at + 1, count)))
            if step < backward:
                ref = block(mod(at + step, count))
                sems[step, -1] = push(ref, ref, target(mod(at - 1, count)))

        def recv(step):
            got = []
            if step < forward:
                owner = mod(at - 1 - step, count)
                arrive(block(owner), sems[step, 1])
                got.append(owner)
            if step < backward:
                owner = mod(at + 1 + step, count)
                arrive(block(owner), sems[step, -1])
                got.append(owner)
            return got

        return send, recv, max(forward, backward)

    first = seqs // 2
    near = pl.ds(0, first)
    far = pl.ds(first, seqs - first)
    other = CORES - 1 - core

    def block_at(part, z_at, y_at):
        return rows_all.at[part, lax.rem(z_at, nt), lax.div(z_at, nt), y_at, core]

    def dev_y(y_at):
        return dev(y_at, z, core)

    def share(part, z_at):
        ref = rows_all.at[part, lax.rem(z_at, nt), lax.div(z_at, nt), :, core]
        sem = push(ref, ref, sibling)
        return rows_all.at[part, lax.rem(z_at, nt), lax.div(z_at, nt), :, other], sem

    shared_near = []
    shared_far = []
    act_sems = []
    steps_up = nz // 2
    steps_down = (nz - 1) // 2
    near_ring = ring(z, nz, lambda z_at: block_at(near, z_at, y), dev_z, steps_up, steps_down)
    far_rings = []
    for d in range(ny):
        y_at = mod(y - d, ny)
        ups, downs = (steps_up, steps_down) if d % 2 else (steps_down, steps_up)
        far_rings.append(
            ring(z, nz, functools.partial(lambda y_at, z_at: block_at(far, z_at, y_at), y_at), dev_z, ups, downs)
        )
    ring_steps = max(steps_up, steps_down)

    def spread_y(z_at):
        ref = block_at(near, z_at, y)
        return z_at, [push(ref, ref, dev_y(mod(y + d, ny))) for d in range(1, ny)]

    def finish_near(owner, sems):
        for d, sem in zip(range(1, ny), sems):
            arrive(block_at(near, owner, mod(y - d, ny)), sem)
        shared_near.append(share(near, owner))

    def prepare_actions():
        for d in range(1, nyk):
            arrive(act_slots.at[:, mod(yk - d, nyk)], act_sems[d - 1])
        act_part = act_slots.shape[3]
        gathered = jnp.zeros((16, act_weight.shape[0]), f32)
        lane = iota((act_part, act_weight.shape[0]), 1)
        lane_row = iota((act_part, act_weight.shape[0]), 0)
        for zh_at in range(HALVES):
            for yk_at in range(nyk):
                c = (yk_at // CORES * HALVES + zh_at) * CORES + yk_at % CORES
                place = (lane == lane_row + c * act_len) & (lane_row < act_len)
                gathered += dot(act_slots[zh_at, yk_at], place.astype(f32).astype(bf16))

        loads[1].wait()
        embedded[...] = dot(gathered.astype(bf16), act_weight[...])

    pl.semaphore_wait(barrier, nz - 1 + nyk - 1)
    loads[0].wait()
    near_send, near_recv, _ = near_ring
    near_send(0)
    far_rings[0][0](0)
    far_y = []
    for d in range(1, ny):
        ref = block_at(far, z, y)
        far_y.append(push(ref, ref, dev_y(mod(y + d, ny))))
    loads[6].wait()
    act_pad[...] = jnp.zeros_like(act_pad)
    act_pad[0:seqs, 0:act_len] = act_raw[...].astype(f32)
    act_slots[zh, yk] = act_pad[...].astype(bf16)
    act_sem = push(act_slots.at[zh, yk], act_slots.at[zh, yk], dev_z(mod(z + nt, nz)))
    waiting = [spread_y(z)]
    rest = far_rings[1:]
    owners_at = {}

    def lead_step(step):
        got = near_recv(step)
        if step + 1 < ring_steps:
            near_send(step + 1)
        owners_at[step] = far_rings[0][1](step)
        if step + 1 < ring_steps:
            far_rings[0][0](step + 1)
        waiting.extend(spread_y(owner) for owner in got)

    def rest_step(step):
        owners = owners_at[step]
        for send, recv, _ in rest:
            got = recv(step)
            if step + 1 < ring_steps:
                send(step + 1)
            owners = got if len(got) > len(owners) else owners
        if step + 1 < ring_steps or steps_up == steps_down:
            shared_far.extend(share(far, owner) for owner in owners)
        else:
            shared_far.append(share(far, mod(z + ring_steps, nz)))

    def finish_waiting(count):
        for item in waiting[:count]:
            finish_near(*item)
        del waiting[:count]

    lead_step(0)
    for d in range(1, ny):
        arrive(block_at(far, z, mod(y - d, ny)), far_y[d - 1])
        far_rings[d][0](0)
    shared_far.append(share(far, z))
    for step in range(ring_steps):
        if step + 1 < ring_steps:
            lead_step(step + 1)
        rest_step(step)
        if step == 0:
            arrive(act_slots.at[1 - zh, yk], act_sem)
            for d in range(1, nyk):
                ref = act_slots.at[:, yk]
                act_sems.append(push(ref, ref, dev_yk(mod(yk + d, nyk))))
            finish_waiting(1)
        else:
            finish_waiting(2)
        if step == 1:
            prepare_actions()
    finish_waiting(len(waiting))

    def position(index):
        zh_at = lax.div(index, half)
        yk_at = lax.div(lax.rem(index, half), steps)
        c = (lax.div(yk_at, CORES) * HALVES + zh_at) * CORES + lax.rem(yk_at, CORES)
        return c * steps + lax.rem(index, steps)

    for load in loads[2:4] + loads[7:]:
        load.wait()
    lane_pos = position(iota((16, hist), 1))
    row_pos = position(iota((hist, 128), 0))

    last_f32[...] = jnp.zeros_like(last_f32)
    for dst, sem in shared_near + shared_far:
        arrive(dst, sem)
    for b in range(seqs):
        pick = (lane_pos == len_ref[b] - 1).astype(f32).astype(bf16)
        own = [dot(pick, rows_all[b, g].reshape(hist, feats)) for g in range(nt)]
        full = jnp.concatenate(own, axis=1)[0:1] + embedded[b : b + 1, :]
        last_f32[b : b + 1, :] = full
    last_rows = last_f32[...]
    last_round = last_rows.astype(bf16).astype(f32)
    last_bf[...] = jnp.concatenate([last_round, jnp.zeros_like(last_round)], axis=0).astype(bf16)
    loads[4].wait()
    query = dot(last_bf[...], weights[0])[0:8]
    row_id = iota((rows, inner), 0)
    row_head = lax.rem(row_id, heads) == lax.div(iota((rows, inner), 1), HEAD_DIM)

    def spread(x):
        out = jnp.zeros((rows, inner), f32)
        for b in range(seqs):
            out = jnp.where((lax.div(row_id, heads) == b) & row_head, x[b : b + 1, :], out)
        return out

    def fold(x):
        shape = x.shape
        seq_of = lax.div(iota(shape, 0), heads)
        out_row = iota((8, shape[1]), 0)
        out = jnp.zeros((8, shape[1]), f32)
        for b in range(seqs):
            total = jnp.sum(jnp.where(seq_of == b, x, 0.0), axis=0, keepdims=True)
            out = jnp.where(out_row == b, total, out)
        return out

    def per_seq(shape, make):
        seq_of = lax.div(iota(shape, 0), heads)
        out = jnp.zeros(shape, f32)
        for b in range(seqs):
            out = jnp.where(seq_of == b, make(b), out)
        return out

    query_rows = spread(query)
    key_vec = dot_split(query_rows, weights[1], NT_DIMS) * scale
    for g in range(nt):
        fact_a_src[g] = key_vec[:, g * feats : (g + 1) * feats].astype(bf16)
    fact_a[z] = fact_a_src[group]
    a_sems = {}
    for d in far_first:
        to = mod(z + d, nz)
        a_sems[d] = push(fact_a_src.at[lax.rem(to, nt)], fact_a.at[z], dev_z(to))

    def project(b):
        is_last = row_pos == len_ref[b] - 1
        mark = jnp.concatenate([is_last] * (feats // 128), axis=1)
        key_sum = jnp.zeros((hist, inner), f32)
        value_sum = jnp.zeros((hist, inner), f32)
        for g in range(nt):
            cut = slice(g * feats, (g + 1) * feats)
            block = rows_all[b, g].reshape(hist, feats).astype(f32)
            block = jnp.where(mark, last_round[b : b + 1, cut], block).astype(bf16)
            key_sum += dot(block, weights[1, cut, :])
            value_sum += dot(block, weights[2, cut, :])
        keys[b] = key_sum.astype(bf16)
        values[b] = value_sum.astype(bf16)

    for b in range(seqs):
        project(b)

    scores = per_seq((rows, hist), lambda b: dot_split(query_rows, keys[b], NT_DIMS)) * scale
    seq_row = lax.div(iota((rows, hist), 0), heads)
    pos = position(iota((rows, hist), 1))
    length = jnp.zeros((rows, hist), jnp.int32)
    for b in range(seqs):
        length = jnp.where(seq_row == b, len_ref[b], length)
    scores = jnp.where(pos < length, scores, -1e30)
    weight = jnp.exp(scores - jnp.max(scores, axis=1, keepdims=True))
    weight = jnp.where(pos < length, weight, 0.0)
    attention = weight / jnp.sum(weight, axis=1, keepdims=True)
    attention_round = attention.astype(bf16)
    attended = per_seq((rows, inner), lambda b: dot(attention_round, values[b]))
    attended = fold(jnp.where(row_head, attended, 0.0))
    loads[5].wait()
    attended_bf = jnp.concatenate([attended, jnp.zeros_like(attended)], axis=0).astype(bf16)
    head_part = dot(attended_bf, out_weight[...])
    quarter = width // 4
    hid_slots[group] = jnp.concatenate(
        [head_part[0:seqs, j * quarter : (j + 1) * quarter] for j in range(4)], axis=0
    ).astype(bf16)
    hid_sems = []
    for d in range(1, nt):
        to = mod(group + d, nt)
        hid_sems.append(push(hid_slots.at[group], hid_slots.at[group], dev_z(zh * nt + to)))

    for h in range(HALVES):
        fact_c_src[h] = attention_round[:, h * half : (h + 1) * half]
    fact_c[z] = fact_c_src[zh]
    c_sems = {}
    for d in far_first:
        to = mod(z + d, nz)
        c_sems[d] = push(fact_c_src.at[lax.div(to, nt)], fact_c.at[z], dev_z(to))

    for d in range(1, nt):
        arrive(hid_slots.at[mod(group - d, nt)], hid_sems[d - 1])
    total = hid_slots[0].astype(f32)
    for g in range(1, nt):
        total = total + hid_slots[g].astype(f32)
    zero_rows = jnp.zeros((8 - seqs, width), f32)
    head_sum = jnp.concatenate([total[j * seqs : (j + 1) * seqs] for j in range(4)], axis=1)
    hidden = last_rows + jnp.concatenate([head_sum, zero_rows], axis=0)
    gain_head = gain_ref[...] * head_ref[...]
    inverse = lax.rsqrt(jnp.sum(hidden * hidden, axis=1, keepdims=True) * (1.0 / width) + NORM_EPS)
    normed = hidden * inverse
    q_vals = jnp.sum(gain_head * normed, axis=1, keepdims=True)
    q_lane = iota((8, 128), 1)
    q_row = iota((8, 128), 0)
    q_line = jnp.sum(jnp.where(q_lane == q_row, q_vals, 0.0), axis=0, keepdims=True)
    boot = jnp.zeros((8, 1), f32)
    for b in range(seqs):
        boot = jnp.where(iota((8, 1), 0) == b, boot_ref[0, b].astype(f32), boot)
    grad_normed = boot * gain_head
    mean = jnp.sum(grad_normed * normed, axis=1, keepdims=True) * (1.0 / width)
    grad_last = inverse * (grad_normed - normed * mean)

    grad_heads = spread(dot_split(grad_last, out_weight[...], NT_DIMS))
    value_vec = dot_split(grad_heads, weights[2], NT_DIMS)
    grad_attention = per_seq((rows, hist), lambda b: dot_split(grad_heads, values[b], NT_DIMS))
    grad_scores = attention * (
        grad_attention - jnp.sum(attention * grad_attention, axis=1, keepdims=True)
    )
    for z_at in range(nz):
        g = z_at % nt
        h = z_at // nt
        fact_b_src[z_at, :, :feats] = value_vec[:, g * feats : (g + 1) * feats].astype(bf16)
        fact_b_src[z_at, :, feats:] = grad_scores[:, h * half : (h + 1) * half].astype(bf16)
    fact_b[z] = fact_b_src[z]
    b_sems = {}
    for d in far_first:
        to = mod(z + d, nz)
        b_sems[d] = (push(fact_b_src.at[to], fact_b.at[z], dev_z(to)))

    grad_query = per_seq((rows, inner), lambda b: dot_split(grad_scores, keys[b]))
    grad_query = fold(jnp.where(row_head, grad_query, 0.0)) * scale
    from_query = dot_split(grad_query, weights[0], NT_DIMS)
    extra_rows = from_query + jnp.where(group == 0, 1.0, 0.0) * grad_last
    at_last = pos == length - 1
    score_last = jnp.sum(jnp.where(at_last, grad_scores, 0.0), axis=1, keepdims=True)
    weight_last = jnp.sum(
        jnp.where(at_last, attention_round.astype(f32), 0.0), axis=1, keepdims=True
    )
    grad_lastrow = extra_rows + fold(score_last * key_vec + weight_last * value_vec)
    act_terms = dot_split(grad_lastrow, act_weight[...], NT_DIMS)
    act_cols = dot_exact(act_terms, act_pick[...])
    cut = feats // 2
    for z_at in range(nz):
        g = z_at % nt
        extra_src[z_at, 0:seqs, :cut] = extra_rows[0:seqs, g * feats : g * feats + cut]
        extra_src[z_at, seqs : 2 * seqs, :cut] = extra_rows[0:seqs, g * feats + cut : (g + 1) * feats]
        extra_src[z_at, :, cut:] = act_cols[:, z_at * 128 : (z_at + 1) * 128]
    extra[z] = extra_src[z]
    x_sems = {}
    for d in far_first:
        to = mod(z + d, nz)
        x_sems[d] = (push(extra_src.at[to], extra.at[z], dev_z(to)))

    for d in range(1, nz):
        arrive(fact_a.at[mod(z - d, nz)], a_sems[d])
        arrive(fact_c.at[mod(z - d, nz)], c_sems[d])
    for d in range(1, nz):
        arrive(fact_b.at[mod(z - d, nz)], b_sems[d])
    factors = nz * rows
    vec_a = fact_a[...].reshape(factors, feats)
    vec_b = fact_b[:, :, :feats].reshape(factors, feats)
    coef_a = fact_b[:, :, feats:].reshape(factors, half).astype(f32)
    coef_b = fact_c[...].reshape(factors, half).astype(f32)
    coefs = jnp.concatenate([coef_a.T, coef_b.T], axis=1)
    vecs = jnp.concatenate([vec_a, vec_b], axis=0)
    seq_col = lax.div(lax.rem(iota(coefs.shape, 1), rows), heads)
    y_sems = {}
    sib_sems = {}

    def multiply(b):
        out = dot(jnp.where(seq_col == b, coefs, 0.0).astype(bf16), vecs)
        partial[b] = out.reshape(ny, CORES, steps, feats)
        sib_sems[b] = push(partial.at[b, :, other], sib_part.at[b], sibling)

    def over_y(b):
        arrive(sib_part.at[b], sib_sems[b])
        total = partial[b, :, core] + sib_part[b]
        row_sum[b] = total
        row_send[b] = total.astype(bf16)
        for d in range(1, ny):
            y_sems[b, d] = push(
                row_send.at[b, mod(y + d, ny)], row_parts.at[d - 1, b], dev_y(mod(y + d, ny))
            )

    multiply(0)
    multiply(1)
    over_y(0)
    multiply(2)
    over_y(1)
    for d in range(1, nz):
        arrive(extra.at[mod(z - d, nz)], x_sems[d])
    extra_sum = extra[0]
    for z_at in range(1, nz):
        extra_sum = extra_sum + extra[z_at]
    act_sum[yk] = extra_sum
    act_sems = []
    for d in range(1, nyk):
        act_sems.append(push(act_sum.at[yk], act_sum.at[yk], dev_yk(mod(yk + d, nyk))))
    multiply(3)
    over_y(2)
    over_y(3)

    for d in range(1, nyk):
        arrive(act_sum.at[mod(yk - d, nyk)], act_sems[d - 1])
    act_total = act_sum[0]
    for yk_at in range(1, nyk):
        act_total = act_total + act_sum[yk_at]
    mine = (iota((128, 128), 0) == iota((128, 128), 1) + yk * part) & (iota((128, 128), 1) < part)
    act_mine = dot_exact(act_total[:, cut:], mine.astype(f32).astype(bf16))
    out_ref[seqs * steps :, 0:128] = jnp.where(iota((8, 128), 0) == 0, q_line, 0.0)
    out_ref[seqs * steps :, 128:256] = act_mine
    here = iota((steps, feats), 0) + critic * steps
    for b in range(seqs):
        low = jnp.concatenate([act_total[b : b + 1, :cut], act_total[seqs + b : seqs + b + 1, :cut]], axis=1)
        result = row_sum[b, y] + jnp.where(here == len_ref[b] - 1, low, 0.0)
        for d in range(1, ny):
            arrive(row_parts.at[d - 1, b], y_sems[b, d])
            result = result + row_parts[d - 1, b].astype(f32)
        out_ref[b * steps : (b + 1) * steps, :] = result
    for copy in sends:
        copy.wait_send()


def unpack(packed, q_ref, grad_ref, actgrad_ref):
    seqs, steps, feats = grad_ref.shape
    tail = seqs * steps
    q_ref[...] = packed[tail : tail + 1, 0:seqs]
    grad_ref[...] = packed[0:tail, :].reshape(seqs, steps, feats)
    actgrad_ref[...] = packed[tail : tail + seqs, 128 : 128 + actgrad_ref.shape[1]]


def solution(mesh):
    nt = mesh.shape["tensor"]
    ny = mesh.shape["critic"] // (HALVES * CORES)
    nz = HALVES * nt
    nyk = ny * CORES

    def on_device(obs, actions, lengths, boot, project, out_weight, act_weight, gain, head):
        seqs, steps, feats = obs.shape
        width, inner = project.shape[1], project.shape[3]
        act_len = actions.shape[1]
        rows = seqs * (inner // HEAD_DIM)
        hist = steps * HALVES * nyk
        half = steps * nyk
        weights = jnp.transpose(project[0], (1, 0, 2))
        vmem = pl.BlockSpec(memory_space=pltpu.VMEM)
        hbm = pl.BlockSpec(memory_space=pltpu.HBM)
        part = act_len // nt
        flops = 4 * seqs * hist * width * inner
        packed = pl.pallas_call(
            functools.partial(kernel, (ny, nt, seqs, steps, feats, inner, act_len)),
            out_shape=jax.ShapeDtypeStruct((seqs * steps + 8, feats), f32),
            in_specs=[hbm] * 9,
            out_specs=vmem,
            scratch_shapes=[
                pltpu.VMEM((seqs, nt, HALVES, ny, CORES, steps, feats), bf16),
                pltpu.VMEM((3, width, inner), bf16),
                pltpu.VMEM((inner, width), bf16),
                pltpu.VMEM(act_weight.shape[1:], bf16),
                pltpu.VMEM((HALVES, nyk, 16, 128), bf16),
                pltpu.VMEM((seqs, hist, inner), bf16),
                pltpu.VMEM((seqs, hist, inner), bf16),
                pltpu.VMEM((16, width), f32),
                pltpu.VMEM((8, width), f32),
                pltpu.VMEM((16, width), bf16),
                pltpu.VMEM((nt, 16, width // 4), bf16),
                pltpu.VMEM((nt, rows, feats), bf16),
                pltpu.VMEM((nz, rows, feats), bf16),
                pltpu.VMEM((HALVES, rows, half), bf16),
                pltpu.VMEM((nz, rows, half), bf16),
                pltpu.VMEM((nz, rows, feats + half), bf16),
                pltpu.VMEM((nz, rows, feats + half), bf16),
                pltpu.VMEM((nz, 8, feats // 2 + 128), f32),
                pltpu.VMEM((nz, 8, feats // 2 + 128), f32),
                pltpu.VMEM((seqs, ny, CORES, steps, feats), f32),
                pltpu.VMEM((seqs, ny, steps, feats), f32),
                pltpu.VMEM((seqs, ny, steps, feats), f32),
                pltpu.VMEM((seqs, ny, steps, feats), bf16),
                pltpu.VMEM((ny - 1, seqs, steps, feats), bf16),
                pltpu.VMEM((act_weight.shape[1], nz * 128), bf16),
                pltpu.VMEM((nyk, 8, feats // 2 + 128), f32),
                pltpu.VMEM((seqs, act_len), bf16),
                pltpu.VMEM((16, 128), f32),
                pltpu.SMEM((seqs,), jnp.int32),
                pltpu.SMEM((1, seqs), jnp.int32),
                pltpu.VMEM((1, width), f32),
                pltpu.VMEM((1, width), f32),
                pltpu.SemaphoreType.DMA((11,)),
                pltpu.SemaphoreType.DMA((160,)),
                pltpu.SemaphoreType.DMA((160,)),
            ],
            compiler_params=pltpu.CompilerParams(
                collective_id=0, has_side_effects=True, vmem_limit_bytes=63 * 1024 * 1024
            ),
            cost_estimate=pl.CostEstimate(
                flops=flops, bytes_accessed=10 * 1024 * 1024, transcendentals=seqs * hist
            ),
        )(obs, actions, lengths, boot, weights, out_weight[0], act_weight[0], gain, head)
        return pl.pallas_call(
            unpack,
            out_shape=(
                jax.ShapeDtypeStruct((1, seqs), f32),
                jax.ShapeDtypeStruct((seqs, steps, feats), f32),
                jax.ShapeDtypeStruct((seqs, part), f32),
            ),
            in_specs=[vmem],
            out_specs=(vmem, vmem, vmem),
        )(packed)

    in_specs = (
        P("seq", "critic", "tensor"),
        P("seq", "critic"),
        P("seq"),
        P("critic", "seq"),
        P("critic", None, None, "tensor"),
        P("critic", "tensor", None),
        P("critic", None, None),
        P("critic", None),
        P("critic", None),
    )
    out_specs = (P("critic", "seq"), P("seq", "critic", "tensor"), P("seq", ("critic", "tensor")))
    return jax.shard_map(
        on_device, mesh=mesh, in_specs=in_specs, out_specs=out_specs, check_vma=False
    )
```

```python
import functools

import jax
import jax.numpy as jnp
from jax import lax
from jax.experimental import pallas as pl
from jax.experimental.pallas import tpu as pltpu
from jax.sharding import PartitionSpec as P

HEAD_DIM = 128
NORM_EPS = 1e-05
CORES = 2
HALVES = 2

f32 = jnp.float32
bf16 = jnp.bfloat16
NN = (((1,), (0,)), ((), ()))
NT_DIMS = (((1,), (1,)), ((), ()))


def mod(value, count):
    return lax.rem(value + count, count)


def iota(shape, axis):
    return lax.broadcasted_iota(jnp.int32, shape, axis)


def split(x):
    high = x.astype(bf16).astype(f32)
    return jnp.concatenate([high, x - high], axis=0).astype(bf16)


def dot(x, w, dims=NN):
    return lax.dot_general(x, w, dims, preferred_element_type=f32)


def dot_split(x, w, dims=NN):
    rows = x.shape[0]
    both = dot(split(x), w, dims)
    return both[:rows] + both[rows:]


def dot_exact(x, w):
    rows = x.shape[0]
    high = x.astype(bf16).astype(f32)
    rest = x - high
    mid = rest.astype(bf16).astype(f32)
    terms = jnp.concatenate([high, mid, rest - mid], axis=0).astype(bf16)
    out = dot(terms, w)
    return out[:rows] + out[rows : 2 * rows] + out[2 * rows :]


def kernel(
    cfg,
    obs_hbm,
    act_hbm,
    len_hbm,
    boot_hbm,
    project_hbm,
    out_hbm,
    actw_hbm,
    gain_hbm,
    head_hbm,
    out_ref,
    rows_all,
    weights,
    out_weight,
    act_weight,
    act_ring,
    act_slots,
    keys,
    values,
    embedded,
    last_f32,
    last_bf,
    hid_slots,
    fact_a_src,
    fact_a,
    fact_c_src,
    fact_c,
    fact_b_src,
    fact_b,
    extra_src,
    extra,
    partial,
    sib_part,
    row_sum,
    row_send,
    row_parts,
    act_pick,
    act_sum,
    act_raw,
    act_pad,
    len_ref,
    boot_ref,
    gain_ref,
    head_ref,
    local_sem,
    send_sem,
    recv_sem,
):
    ny, nt, seqs, steps, feats, inner, act_len = cfg
    nz = HALVES * nt
    nyk = ny * CORES
    heads = inner // HEAD_DIM
    rows = seqs * heads
    width = nt * feats
    hist = HALVES * nyk * steps
    half = nyk * steps
    scale = HEAD_DIM ** (-0.5)

    critic = lax.axis_index("critic")
    group = lax.axis_index("tensor")
    y = lax.div(critic, HALVES * CORES)
    zh = lax.rem(lax.div(critic, CORES), HALVES)
    core = lax.rem(critic, CORES)
    z = zh * nt + group
    yk = y * CORES + core

    def dev(y_at, z_at, core_at):
        return {
            "critic": (y_at * HALVES + lax.div(z_at, nt)) * CORES + core_at,
            "tensor": lax.rem(z_at, nt),
        }

    def dev_z(z_at):
        return dev(y, z_at, core)

    def dev_yk(yk_at):
        return dev(lax.div(yk_at, CORES), z, lax.rem(yk_at, CORES))

    sibling = dev(y, z, CORES - 1 - core)

    far_first = sorted(range(1, nz), key=lambda d: -min(d, nz - d))

    loads = [
        pltpu.make_async_copy(src, dst, local_sem.at[i])
        for i, (src, dst) in enumerate(
            [
                (obs_hbm, rows_all.at[:, group, zh, y, core]),
                (actw_hbm, act_weight),
                (project_hbm.at[1], weights.at[1]),
                (project_hbm.at[2], weights.at[2]),
                (project_hbm.at[0], weights.at[0]),
                (out_hbm, out_weight),
                (act_hbm, act_raw),
                (len_hbm, len_ref),
                (boot_hbm, boot_ref),
                (gain_hbm, gain_ref),
                (head_hbm, head_ref),
            ]
        )
    ]
    for load in loads:
        load.start()

    barrier = pltpu.get_barrier_semaphore()
    greeted = [dev_z(mod(z + d, nz)) for d in sorted({1, nz - 1})]
    greeted += [dev(mod(y + d, ny), z, core) for d in range(1, ny)] + [sibling]
    for target in greeted:
        pl.semaphore_signal(barrier, inc=1, device_id=target, device_id_type=pl.DeviceIdType.MESH)

    part = act_len // nt
    pick_shape = act_pick.shape
    col = iota(pick_shape, 1)
    row = iota(pick_shape, 0)
    to_z = lax.div(col, 128)
    within = lax.rem(col, 128)
    to_yk = lax.div(within, part)
    to_critic = (lax.div(to_yk, CORES) * HALVES + lax.div(to_z, nt)) * CORES + lax.rem(to_yk, CORES)
    source = (to_critic * nt + lax.rem(to_z, nt)) * part + lax.rem(within, part)
    act_pick[...] = ((row == source) & (within < nyk * part)).astype(f32).astype(bf16)

    sends = []
    sem_at = [0]

    def drain(count):
        for copy in sends[:count]:
            copy.wait_send()
        del sends[:count]

    def copy_of(src, dst, target, sem):
        return pltpu.make_async_remote_copy(
            src_ref=src,
            dst_ref=dst,
            send_sem=send_sem.at[sem],
            recv_sem=recv_sem.at[sem],
            device_id=target,
            device_id_type=pl.DeviceIdType.MESH,
        )

    def push(src, dst, target):
        sem = sem_at[0]
        sem_at[0] += 1
        copy = copy_of(src, dst, target, sem)
        copy.start()
        sends.append(copy)
        return sem

    def arrive(dst, sem):
        copy_of(dst, dst, sibling, sem).wait_recv()

    def ring(at, count, block, target, forward, backward):
        sems = {}

        def send(step):
            if step < forward:
                ref = block(mod(at - step, count))
                sems[step, 1] = push(ref, ref, target(mod(at + 1, count)))
            if step < backward:
                ref = block(mod(at + step, count))
                sems[step, -1] = push(ref, ref, target(mod(at - 1, count)))

        def recv(step):
            got = []
            if step < forward:
                owner = mod(at - 1 - step, count)
                arrive(block(owner), sems[step, 1])
                got.append(owner)
            if step < backward:
                owner = mod(at + 1 + step, count)
                arrive(block(owner), sems[step, -1])
                got.append(owner)
            return got

        return send, recv, max(forward, backward)

    first = seqs // 2
    near = pl.ds(0, first)
    far = pl.ds(first, seqs - first)
    other = CORES - 1 - core

    def block_at(part, z_at, y_at):
        return rows_all.at[part, lax.rem(z_at, nt), lax.div(z_at, nt), y_at, core]

    def dev_y(y_at):
        return dev(y_at, z, core)

    def share(part, z_at):
        ref = rows_all.at[part, lax.rem(z_at, nt), lax.div(z_at, nt), :, core]
        sem = push(ref, ref, sibling)
        return rows_all.at[part, lax.rem(z_at, nt), lax.div(z_at, nt), :, other], sem

    shared_near = []
    shared_far = []
    act_sems = []
    steps_up = nz // 2
    steps_down = (nz - 1) // 2
    near_ring = ring(z, nz, lambda z_at: block_at(near, z_at, y), dev_z, steps_up, steps_down)
    near_first = sorted(range(1, ny), key=lambda d: min(d, ny - d))
    far_rings = {}
    for d in range(ny):
        y_at = mod(y - d, ny)
        ups, downs = (steps_up, steps_down) if d % 2 else (steps_down, steps_up)
        far_rings[d] = (
            ring(z, nz, functools.partial(lambda y_at, z_at: block_at(far, z_at, y_at), y_at), dev_z, ups, downs)
        )
    ring_steps = max(steps_up, steps_down)

    def spread_y(z_at):
        ref = block_at(near, z_at, y)
        return z_at, [push(ref, ref, dev_y(mod(y + d, ny))) for d in range(1, ny)]

    def finish_near(owner, sems):
        for d, sem in zip(range(1, ny), sems):
            arrive(block_at(near, owner, mod(y - d, ny)), sem)
        shared_near.append(share(near, owner))

    def prepare_actions():
        act_part = act_slots.shape[4]
        gathered = jnp.zeros((16, act_weight.shape[0]), f32)
        lane = iota((act_part, act_weight.shape[0]), 1)
        lane_row = iota((act_part, act_weight.shape[0]), 0)
        for zh_at in range(HALVES):
            for yk_at in range(nyk):
                c = (yk_at // CORES * HALVES + zh_at) * CORES + yk_at % CORES
                place = (lane == lane_row + c * act_len) & (lane_row < act_len)
                gathered += dot(act_slots[zh_at, yk_at // CORES, yk_at % CORES], place.astype(f32).astype(bf16))

        loads[1].wait()
        embedded[...] = dot(gathered.astype(bf16), act_weight[...])

    pl.semaphore_wait(barrier, len(greeted))
    loads[0].wait()
    near_send, near_recv, _ = near_ring
    near_send(0)
    far_rings[0][0](0)
    far_y = []
    for d in range(1, ny):
        ref = block_at(far, z, y)
        far_y.append(push(ref, ref, dev_y(mod(y + d, ny))))
    loads[6].wait()
    act_pad[...] = jnp.zeros_like(act_pad)
    act_pad[0:seqs, 0:act_len] = act_raw[...].astype(f32)
    act_ring[z] = act_pad[...].astype(bf16)
    act_sem = {}

    def act_step(step):
        if step > 0:
            arrive(act_ring.at[mod(z - step, nz)], act_sem[step - 1])
        if step < nt:
            ref = act_ring.at[mod(z - step, nz)]
            act_sem[step] = push(ref, ref, dev_z(mod(z + 1, nz)))

    act_step(0)
    waiting = [spread_y(z)]
    rest = [far_rings[d] for d in near_first]
    owners_at = {}

    def lead_step(step):
        got = near_recv(step)
        if step + 1 < ring_steps:
            near_send(step + 1)
        owners_at[step] = far_rings[0][1](step)
        if step + 1 < ring_steps:
            far_rings[0][0](step + 1)
        act_step(step + 1)
        waiting.extend(spread_y(owner) for owner in got)

    def rest_step(step):
        owners = owners_at[step]
        for send, recv, _ in rest:
            got = recv(step)
            if step + 1 < ring_steps:
                send(step + 1)
            owners = got if len(got) > len(owners) else owners
        if step + 1 < ring_steps or steps_up == steps_down:
            shared_far.extend(share(far, owner) for owner in owners)
        else:
            shared_far.append(share(far, mod(z + ring_steps, nz)))

    def finish_waiting(count):
        for item in waiting[:count]:
            finish_near(*item)
        del waiting[:count]

    lead_step(0)
    for d in near_first:
        arrive(block_at(far, z, mod(y - d, ny)), far_y[d - 1])
        far_rings[d][0](0)
    shared_far.append(share(far, z))
    for step in range(ring_steps):
        if step + 1 < ring_steps:
            lead_step(step + 1)
        rest_step(step)
        if step + 2 == ring_steps:
            act_slots[zh, y, core] = act_ring[z]
            act_slots[1 - zh, y, core] = act_ring[mod(z - nt, nz)]
            for d in range(1, ny):
                ref = act_slots.at[:, y, core]
                act_sems.append(push(ref, ref, dev_y(mod(y + d, ny))))
        finish_waiting(1 if step == 0 else 2)
    for d in range(1, ny):
        arrive(act_slots.at[:, mod(y - d, ny), core], act_sems[d - 1])
    act_share = push(act_slots.at[:, :, core], act_slots.at[:, :, core], sibling)
    finish_waiting(len(waiting))
    arrive(act_slots.at[:, :, other], act_share)
    prepare_actions()

    def position(index):
        zh_at = lax.div(index, half)
        yk_at = lax.div(lax.rem(index, half), steps)
        c = (lax.div(yk_at, CORES) * HALVES + zh_at) * CORES + lax.rem(yk_at, CORES)
        return c * steps + lax.rem(index, steps)

    for load in loads[2:4] + loads[7:]:
        load.wait()
    lane_pos = position(iota((16, hist), 1))
    row_pos = position(iota((hist, 128), 0))

    last_f32[...] = jnp.zeros_like(last_f32)
    for dst, sem in shared_near + shared_far:
        arrive(dst, sem)
    for b in range(seqs):
        pick = (lane_pos == len_ref[b] - 1).astype(f32).astype(bf16)
        own = [dot(pick, rows_all[b, g].reshape(hist, feats)) for g in range(nt)]
        full = jnp.concatenate(own, axis=1)[0:1] + embedded[b : b + 1, :]
        last_f32[b : b + 1, :] = full
    last_rows = last_f32[...]
    last_round = last_rows.astype(bf16).astype(f32)
    last_bf[...] = jnp.concatenate([last_round, jnp.zeros_like(last_round)], axis=0).astype(bf16)
    loads[4].wait()
    query = dot(last_bf[...], weights[0])[0:8]
    row_id = iota((rows, inner), 0)
    row_head = lax.rem(row_id, heads) == lax.div(iota((rows, inner), 1), HEAD_DIM)

    def spread(x):
        out = jnp.zeros((rows, inner), f32)
        for b in range(seqs):
            out = jnp.where((lax.div(row_id, heads) == b) & row_head, x[b : b + 1, :], out)
        return out

    def fold(x):
        shape = x.shape
        seq_of = lax.div(iota(shape, 0), heads)
        out_row = iota((8, shape[1]), 0)
        out = jnp.zeros((8, shape[1]), f32)
        for b in range(seqs):
            total = jnp.sum(jnp.where(seq_of == b, x, 0.0), axis=0, keepdims=True)
            out = jnp.where(out_row == b, total, out)
        return out

    def per_seq(shape, make):
        seq_of = lax.div(iota(shape, 0), heads)
        out = jnp.zeros(shape, f32)
        for b in range(seqs):
            out = jnp.where(seq_of == b, make(b), out)
        return out

    query_rows = spread(query)
    key_vec = dot_split(query_rows, weights[1], NT_DIMS) * scale
    for g in range(nt):
        fact_a_src[g] = key_vec[:, g * feats : (g + 1) * feats].astype(bf16)
    fact_a[z] = fact_a_src[group]
    a_sems = {}
    for d in far_first:
        to = mod(z + d, nz)
        a_sems[d] = push(fact_a_src.at[lax.rem(to, nt)], fact_a.at[z], dev_z(to))

    def project(b):
        is_last = row_pos == len_ref[b] - 1
        mark = jnp.concatenate([is_last] * (feats // 128), axis=1)
        key_sum = jnp.zeros((hist, inner), f32)
        value_sum = jnp.zeros((hist, inner), f32)
        for g in range(nt):
            cut = slice(g * feats, (g + 1) * feats)
            block = rows_all[b, g].reshape(hist, feats).astype(f32)
            block = jnp.where(mark, last_round[b : b + 1, cut], block).astype(bf16)
            key_sum += dot(block, weights[1, cut, :])
            value_sum += dot(block, weights[2, cut, :])
        keys[b] = key_sum.astype(bf16)
        values[b] = value_sum.astype(bf16)

    for b in range(seqs):
        project(b)

    scores = per_seq((rows, hist), lambda b: dot_split(query_rows, keys[b], NT_DIMS)) * scale
    seq_row = lax.div(iota((rows, hist), 0), heads)
    pos = position(iota((rows, hist), 1))
    length = jnp.zeros((rows, hist), jnp.int32)
    for b in range(seqs):
        length = jnp.where(seq_row == b, len_ref[b], length)
    scores = jnp.where(pos < length, scores, -1e30)
    weight = jnp.exp(scores - jnp.max(scores, axis=1, keepdims=True))
    weight = jnp.where(pos < length, weight, 0.0)
    attention = weight / jnp.sum(weight, axis=1, keepdims=True)
    attention_round = attention.astype(bf16)
    attended = per_seq((rows, inner), lambda b: dot(attention_round, values[b]))
    attended = fold(jnp.where(row_head, attended, 0.0))
    loads[5].wait()
    attended_bf = jnp.concatenate([attended, jnp.zeros_like(attended)], axis=0).astype(bf16)
    head_part = dot(attended_bf, out_weight[...])
    quarter = width // 4
    hid_slots[group] = jnp.concatenate(
        [head_part[0:seqs, j * quarter : (j + 1) * quarter] for j in range(4)], axis=0
    ).astype(bf16)
    hid_sems = []
    for d in range(1, nt):
        to = mod(group + d, nt)
        hid_sems.append(push(hid_slots.at[group], hid_slots.at[group], dev_z(zh * nt + to)))

    for h in range(HALVES):
        fact_c_src[h] = attention_round[:, h * half : (h + 1) * half]
    fact_c[z] = fact_c_src[zh]
    c_sems = {}
    for d in far_first:
        to = mod(z + d, nz)
        c_sems[d] = push(fact_c_src.at[lax.div(to, nt)], fact_c.at[z], dev_z(to))

    for d in range(1, nz):
        arrive(fact_a.at[mod(z - d, nz)], a_sems[d])
    for d in range(1, nt):
        arrive(hid_slots.at[mod(group - d, nt)], hid_sems[d - 1])
    total = hid_slots[0].astype(f32)
    for g in range(1, nt):
        total = total + hid_slots[g].astype(f32)
    zero_rows = jnp.zeros((8 - seqs, width), f32)
    head_sum = jnp.concatenate([total[j * seqs : (j + 1) * seqs] for j in range(4)], axis=1)
    hidden = last_rows + jnp.concatenate([head_sum, zero_rows], axis=0)
    gain_head = gain_ref[...] * head_ref[...]
    inverse = lax.rsqrt(jnp.sum(hidden * hidden, axis=1, keepdims=True) * (1.0 / width) + NORM_EPS)
    normed = hidden * inverse
    q_vals = jnp.sum(gain_head * normed, axis=1, keepdims=True)
    q_lane = iota((8, 128), 1)
    q_row = iota((8, 128), 0)
    q_line = jnp.sum(jnp.where(q_lane == q_row, q_vals, 0.0), axis=0, keepdims=True)
    boot = jnp.zeros((8, 1), f32)
    for b in range(seqs):
        boot = jnp.where(iota((8, 1), 0) == b, boot_ref[0, b].astype(f32), boot)
    grad_normed = boot * gain_head
    mean = jnp.sum(grad_normed * normed, axis=1, keepdims=True) * (1.0 / width)
    grad_last = inverse * (grad_normed - normed * mean)

    grad_heads = spread(dot_split(grad_last, out_weight[...], NT_DIMS))
    value_vec = dot_split(grad_heads, weights[2], NT_DIMS)
    grad_attention = per_seq((rows, hist), lambda b: dot_split(grad_heads, values[b], NT_DIMS))
    grad_scores = attention * (
        grad_attention - jnp.sum(attention * grad_attention, axis=1, keepdims=True)
    )
    for z_at in range(nz):
        g = z_at % nt
        h = z_at // nt
        fact_b_src[z_at, :, :feats] = value_vec[:, g * feats : (g + 1) * feats].astype(bf16)
        fact_b_src[z_at, :, feats:] = grad_scores[:, h * half : (h + 1) * half].astype(bf16)
    fact_b[z] = fact_b_src[z]
    before_b = len(sends)
    b_sems = {}
    for d in far_first:
        to = mod(z + d, nz)
        b_sems[d] = (push(fact_b_src.at[to], fact_b.at[z], dev_z(to)))

    grad_query = per_seq((rows, inner), lambda b: dot_split(grad_scores, keys[b]))
    grad_query = fold(jnp.where(row_head, grad_query, 0.0)) * scale
    from_query = dot_split(grad_query, weights[0], NT_DIMS)
    extra_rows = from_query + jnp.where(group == 0, 1.0, 0.0) * grad_last
    at_last = pos == length - 1
    score_last = jnp.sum(jnp.where(at_last, grad_scores, 0.0), axis=1, keepdims=True)
    weight_last = jnp.sum(
        jnp.where(at_last, attention_round.astype(f32), 0.0), axis=1, keepdims=True
    )
    grad_lastrow = extra_rows + fold(score_last * key_vec + weight_last * value_vec)
    act_terms = dot_split(grad_lastrow, act_weight[...], NT_DIMS)
    act_cols = dot_exact(act_terms, act_pick[...])
    cut = feats // 2
    for z_at in range(nz):
        g = z_at % nt
        extra_src[z_at, 0:seqs, :cut] = extra_rows[0:seqs, g * feats : g * feats + cut]
        extra_src[z_at, seqs : 2 * seqs, :cut] = extra_rows[0:seqs, g * feats + cut : (g + 1) * feats]
        extra_src[z_at, :, cut:] = act_cols[:, z_at * 128 : (z_at + 1) * 128]
    extra[z] = extra_src[z]
    x_sems = {}
    for d in far_first:
        to = mod(z + d, nz)
        x_sems[d] = (push(extra_src.at[to], extra.at[z], dev_z(to)))

    drain(before_b)
    factors = nz * rows
    for d in range(1, nz):
        arrive(fact_c.at[mod(z - d, nz)], c_sems[d])
    coef_b = fact_c[...].reshape(factors, half).astype(f32).T
    for d in range(1, nz):
        arrive(fact_b.at[mod(z - d, nz)], b_sems[d])
    coef_a = fact_b[:, :, feats:].reshape(factors, half).astype(f32).T
    coefs = jnp.concatenate([coef_a, coef_b], axis=1)
    vecs = jnp.concatenate(
        [fact_a[...].reshape(factors, feats), fact_b[:, :, :feats].reshape(factors, feats)], axis=0
    )
    seq_col = lax.div(lax.rem(iota(coefs.shape, 1), rows), heads)
    y_sems = {}
    sib_sems = {}

    def multiply(b):
        out = dot(jnp.where(seq_col == b, coefs, 0.0).astype(bf16), vecs)
        partial[b] = out.reshape(ny, CORES, steps, feats)
        sib_sems[b] = push(partial.at[b, :, other], sib_part.at[b], sibling)

    def over_y(b):
        arrive(sib_part.at[b], sib_sems[b])
        total = partial[b, :, core] + sib_part[b]
        row_sum[b] = total
        row_send[b] = total.astype(bf16)
        for d in range(1, ny):
            y_sems[b, d] = push(
                row_send.at[b, mod(y + d, ny)], row_parts.at[d - 1, b], dev_y(mod(y + d, ny))
            )

    multiply(0)
    multiply(1)
    over_y(0)
    multiply(2)
    over_y(1)
    for d in range(1, nz):
        arrive(extra.at[mod(z - d, nz)], x_sems[d])
    extra_sum = extra[0]
    for z_at in range(1, nz):
        extra_sum = extra_sum + extra[z_at]
    act_sum[yk] = extra_sum
    act_sems = []
    for d in range(1, nyk):
        act_sems.append(push(act_sum.at[yk], act_sum.at[yk], dev_yk(mod(yk + d, nyk))))
    multiply(3)
    over_y(2)
    over_y(3)
    drain(2 * (nz - 1))

    for d in range(1, nyk):
        arrive(act_sum.at[mod(yk - d, nyk)], act_sems[d - 1])
    act_total = act_sum[0]
    for yk_at in range(1, nyk):
        act_total = act_total + act_sum[yk_at]
    mine = (iota((128, 128), 0) == iota((128, 128), 1) + yk * part) & (iota((128, 128), 1) < part)
    act_mine = dot_exact(act_total[:, cut:], mine.astype(f32).astype(bf16))
    out_ref[seqs * steps :, 0:128] = jnp.where(iota((8, 128), 0) == 0, q_line, 0.0)
    out_ref[seqs * steps :, 128:256] = act_mine
    here = iota((steps, feats), 0) + critic * steps
    for b in range(seqs):
        low = jnp.concatenate([act_total[b : b + 1, :cut], act_total[seqs + b : seqs + b + 1, :cut]], axis=1)
        result = row_sum[b, y] + jnp.where(here == len_ref[b] - 1, low, 0.0)
        for d in range(1, ny):
            arrive(row_parts.at[d - 1, b], y_sems[b, d])
            result = result + row_parts[d - 1, b].astype(f32)
        out_ref[b * steps : (b + 1) * steps, :] = result
    drain(len(sends))


def unpack(packed, q_ref, grad_ref, actgrad_ref):
    seqs, steps, feats = grad_ref.shape
    tail = seqs * steps
    q_ref[...] = packed[tail : tail + 1, 0:seqs]
    grad_ref[...] = packed[0:tail, :].reshape(seqs, steps, feats)
    actgrad_ref[...] = packed[tail : tail + seqs, 128 : 128 + actgrad_ref.shape[1]]


def solution(mesh):
    nt = mesh.shape["tensor"]
    ny = mesh.shape["critic"] // (HALVES * CORES)
    nz = HALVES * nt
    nyk = ny * CORES

    def on_device(obs, actions, lengths, boot, project, out_weight, act_weight, gain, head):
        seqs, steps, feats = obs.shape
        width, inner = project.shape[1], project.shape[3]
        act_len = actions.shape[1]
        rows = seqs * (inner // HEAD_DIM)
        hist = steps * HALVES * nyk
        half = steps * nyk
        weights = jnp.transpose(project[0], (1, 0, 2))
        vmem = pl.BlockSpec(memory_space=pltpu.VMEM)
        hbm = pl.BlockSpec(memory_space=pltpu.HBM)
        part = act_len // nt
        flops = 4 * seqs * hist * width * inner
        packed = pl.pallas_call(
            functools.partial(kernel, (ny, nt, seqs, steps, feats, inner, act_len)),
            out_shape=jax.ShapeDtypeStruct((seqs * steps + 8, feats), f32),
            in_specs=[hbm] * 9,
            out_specs=vmem,
            scratch_shapes=[
                pltpu.VMEM((seqs, nt, HALVES, ny, CORES, steps, feats), bf16),
                pltpu.VMEM((3, width, inner), bf16),
                pltpu.VMEM((inner, width), bf16),
                pltpu.VMEM(act_weight.shape[1:], bf16),
                pltpu.VMEM((nz, 16, 128), bf16),
                pltpu.VMEM((HALVES, ny, CORES, 16, 128), bf16),
                pltpu.VMEM((seqs, hist, inner), bf16),
                pltpu.VMEM((seqs, hist, inner), bf16),
                pltpu.VMEM((16, width), f32),
                pltpu.VMEM((8, width), f32),
                pltpu.VMEM((16, width), bf16),
                pltpu.VMEM((nt, 16, width // 4), bf16),
                pltpu.VMEM((nt, rows, feats), bf16),
                pltpu.VMEM((nz, rows, feats), bf16),
                pltpu.VMEM((HALVES, rows, half), bf16),
                pltpu.VMEM((nz, rows, half), bf16),
                pltpu.VMEM((nz, rows, feats + half), bf16),
                pltpu.VMEM((nz, rows, feats + half), bf16),
                pltpu.VMEM((nz, 8, feats // 2 + 128), f32),
                pltpu.VMEM((nz, 8, feats // 2 + 128), f32),
                pltpu.VMEM((seqs, ny, CORES, steps, feats), f32),
                pltpu.VMEM((seqs, ny, steps, feats), f32),
                pltpu.VMEM((seqs, ny, steps, feats), f32),
                pltpu.VMEM((seqs, ny, steps, feats), bf16),
                pltpu.VMEM((ny - 1, seqs, steps, feats), bf16),
                pltpu.VMEM((act_weight.shape[1], nz * 128), bf16),
                pltpu.VMEM((nyk, 8, feats // 2 + 128), f32),
                pltpu.VMEM((seqs, act_len), bf16),
                pltpu.VMEM((16, 128), f32),
                pltpu.SMEM((seqs,), jnp.int32),
                pltpu.SMEM((1, seqs), jnp.int32),
                pltpu.VMEM((1, width), f32),
                pltpu.VMEM((1, width), f32),
                pltpu.SemaphoreType.DMA((11,)),
                pltpu.SemaphoreType.DMA((160,)),
                pltpu.SemaphoreType.DMA((160,)),
            ],
            compiler_params=pltpu.CompilerParams(
                collective_id=0, has_side_effects=True, vmem_limit_bytes=63 * 1024 * 1024
            ),
            cost_estimate=pl.CostEstimate(
                flops=flops, bytes_accessed=10 * 1024 * 1024, transcendentals=seqs * hist
            ),
        )(obs, actions, lengths, boot, weights, out_weight[0], act_weight[0], gain, head)
        return pl.pallas_call(
            unpack,
            out_shape=(
                jax.ShapeDtypeStruct((1, seqs), f32),
                jax.ShapeDtypeStruct((seqs, steps, feats), f32),
                jax.ShapeDtypeStruct((seqs, part), f32),
            ),
            in_specs=[vmem],
            out_specs=(vmem, vmem, vmem),
        )(packed)

    in_specs = (
        P("seq", "critic", "tensor"),
        P("seq", "critic"),
        P("seq"),
        P("critic", "seq"),
        P("critic", None, None, "tensor"),
        P("critic", "tensor", None),
        P("critic", None, None),
        P("critic", None),
        P("critic", None),
    )
    out_specs = (P("critic", "seq"), P("seq", "critic", "tensor"), P("seq", ("critic", "tensor")))
    return jax.shard_map(
        on_device, mesh=mesh, in_specs=in_specs, out_specs=out_specs, check_vma=False
    )
```

```python
import functools

import jax
import jax.numpy as jnp
from jax import lax
from jax.experimental import pallas as pl
from jax.experimental.pallas import tpu as pltpu
from jax.sharding import PartitionSpec as P

HEAD_DIM = 128
NORM_EPS = 1e-05
CORES = 2
HALVES = 2

f32 = jnp.float32
bf16 = jnp.bfloat16
NN = (((1,), (0,)), ((), ()))
NT_DIMS = (((1,), (1,)), ((), ()))


def mod(value, count):
    return lax.rem(value + count, count)


def iota(shape, axis):
    return lax.broadcasted_iota(jnp.int32, shape, axis)


def split(x):
    high = x.astype(bf16).astype(f32)
    return jnp.concatenate([high, x - high], axis=0).astype(bf16)


def dot(x, w, dims=NN):
    return lax.dot_general(x, w, dims, preferred_element_type=f32)


def dot_split(x, w, dims=NN):
    rows = x.shape[0]
    both = dot(split(x), w, dims)
    return both[:rows] + both[rows:]


def dot_exact(x, w):
    rows = x.shape[0]
    high = x.astype(bf16).astype(f32)
    rest = x - high
    mid = rest.astype(bf16).astype(f32)
    terms = jnp.concatenate([high, mid, rest - mid], axis=0).astype(bf16)
    out = dot(terms, w)
    return out[:rows] + out[rows : 2 * rows] + out[2 * rows :]


def kernel(
    cfg,
    obs_hbm,
    act_hbm,
    len_hbm,
    boot_hbm,
    project_hbm,
    out_hbm,
    actw_hbm,
    gain_hbm,
    head_hbm,
    out_ref,
    rows_all,
    weights,
    out_weight,
    act_weight,
    act_ring,
    act_slots,
    keys,
    values,
    embedded,
    last_f32,
    last_bf,
    hid_slots,
    fact_a_src,
    fact_a,
    fact_c_src,
    fact_c,
    fact_b_src,
    fact_b,
    fact_d_src,
    fact_d,
    extra_src,
    extra,
    partial,
    sib_part,
    row_sum,
    row_send,
    row_parts,
    act_pick,
    act_sum,
    act_raw,
    act_pad,
    len_ref,
    boot_ref,
    gain_ref,
    head_ref,
    local_sem,
    send_sem,
    recv_sem,
):
    ny, nt, seqs, steps, feats, inner, act_len = cfg
    nz = HALVES * nt
    nyk = ny * CORES
    heads = inner // HEAD_DIM
    rows = seqs * heads
    width = nt * feats
    hist = HALVES * nyk * steps
    half = nyk * steps
    scale = HEAD_DIM ** (-0.5)

    critic = lax.axis_index("critic")
    group = lax.axis_index("tensor")
    y = lax.div(critic, HALVES * CORES)
    zh = lax.rem(lax.div(critic, CORES), HALVES)
    core = lax.rem(critic, CORES)
    z = zh * nt + group
    yk = y * CORES + core

    def dev(y_at, z_at, core_at):
        return {
            "critic": (y_at * HALVES + lax.div(z_at, nt)) * CORES + core_at,
            "tensor": lax.rem(z_at, nt),
        }

    def dev_z(z_at):
        return dev(y, z_at, core)

    def dev_yk(yk_at):
        return dev(lax.div(yk_at, CORES), z, lax.rem(yk_at, CORES))

    sibling = dev(y, z, CORES - 1 - core)

    far_first = sorted(range(1, nz), key=lambda d: -min(d, nz - d))

    loads = [
        pltpu.make_async_copy(src, dst, local_sem.at[i])
        for i, (src, dst) in enumerate(
            [
                (obs_hbm, rows_all.at[:, group, zh, y, core]),
                (actw_hbm, act_weight),
                (project_hbm.at[1], weights.at[1]),
                (project_hbm.at[2], weights.at[2]),
                (project_hbm.at[0], weights.at[0]),
                (out_hbm, out_weight),
                (act_hbm, act_raw),
                (len_hbm, len_ref),
                (boot_hbm, boot_ref),
                (gain_hbm, gain_ref),
                (head_hbm, head_ref),
            ]
        )
    ]
    for load in loads:
        load.start()

    barrier = pltpu.get_barrier_semaphore()
    greeted = [dev_z(mod(z + d, nz)) for d in sorted({1, nz - 1})]
    greeted += [dev(mod(y + d, ny), z, core) for d in range(1, ny)] + [sibling]
    for target in greeted:
        pl.semaphore_signal(barrier, inc=1, device_id=target, device_id_type=pl.DeviceIdType.MESH)

    part = act_len // nt
    pick_shape = act_pick.shape
    col = iota(pick_shape, 1)
    row = iota(pick_shape, 0)
    to_z = lax.div(col, 128)
    within = lax.rem(col, 128)
    to_yk = lax.div(within, part)
    to_critic = (lax.div(to_yk, CORES) * HALVES + lax.div(to_z, nt)) * CORES + lax.rem(to_yk, CORES)
    source = (to_critic * nt + lax.rem(to_z, nt)) * part + lax.rem(within, part)
    act_pick[...] = ((row == source) & (within < nyk * part)).astype(f32).astype(bf16)

    sends = []
    sem_at = [0]

    def drain(count):
        for copy in sends[:count]:
            copy.wait_send()
        del sends[:count]

    def copy_of(src, dst, target, sem):
        return pltpu.make_async_remote_copy(
            src_ref=src,
            dst_ref=dst,
            send_sem=send_sem.at[sem],
            recv_sem=recv_sem.at[sem],
            device_id=target,
            device_id_type=pl.DeviceIdType.MESH,
        )

    def push(src, dst, target):
        sem = sem_at[0]
        sem_at[0] += 1
        copy = copy_of(src, dst, target, sem)
        copy.start()
        sends.append(copy)
        return sem

    def arrive(dst, sem):
        copy_of(dst, dst, sibling, sem).wait_recv()

    def ring(at, count, block, target, forward, backward):
        sems = {}

        def send(step):
            if step < forward:
                ref = block(mod(at - step, count))
                sems[step, 1] = push(ref, ref, target(mod(at + 1, count)))
            if step < backward:
                ref = block(mod(at + step, count))
                sems[step, -1] = push(ref, ref, target(mod(at - 1, count)))

        def recv(step):
            got = []
            if step < forward:
                owner = mod(at - 1 - step, count)
                arrive(block(owner), sems[step, 1])
                got.append(owner)
            if step < backward:
                owner = mod(at + 1 + step, count)
                arrive(block(owner), sems[step, -1])
                got.append(owner)
            return got

        return send, recv, max(forward, backward)

    first = seqs // 2
    near = pl.ds(0, first)
    far = pl.ds(first, seqs - first)
    other = CORES - 1 - core

    def block_at(part, z_at, y_at):
        return rows_all.at[part, lax.rem(z_at, nt), lax.div(z_at, nt), y_at, core]

    def dev_y(y_at):
        return dev(y_at, z, core)

    def share(part, z_at):
        ref = rows_all.at[part, lax.rem(z_at, nt), lax.div(z_at, nt), :, core]
        sem = push(ref, ref, sibling)
        return rows_all.at[part, lax.rem(z_at, nt), lax.div(z_at, nt), :, other], sem

    shared_near = []
    shared_far = []
    act_sems = []
    steps_up = nz // 2
    steps_down = (nz - 1) // 2
    near_ring = ring(z, nz, lambda z_at: block_at(near, z_at, y), dev_z, steps_up, steps_down)
    near_first = sorted(range(1, ny), key=lambda d: min(d, ny - d))
    far_rings = {}
    for d in range(ny):
        y_at = mod(y - d, ny)
        ups, downs = (steps_up, steps_down) if d % 2 else (steps_down, steps_up)
        far_rings[d] = (
            ring(z, nz, functools.partial(lambda y_at, z_at: block_at(far, z_at, y_at), y_at), dev_z, ups, downs)
        )
    ring_steps = max(steps_up, steps_down)

    def spread_y(z_at):
        ref = block_at(near, z_at, y)
        return z_at, [push(ref, ref, dev_y(mod(y + d, ny))) for d in range(1, ny)]

    def finish_near(owner, sems):
        for d, sem in zip(range(1, ny), sems):
            arrive(block_at(near, owner, mod(y - d, ny)), sem)
        shared_near.append(share(near, owner))

    def prepare_actions():
        act_part = act_slots.shape[4]
        gathered = jnp.zeros((16, act_weight.shape[0]), f32)
        lane = iota((act_part, act_weight.shape[0]), 1)
        lane_row = iota((act_part, act_weight.shape[0]), 0)
        for zh_at in range(HALVES):
            for yk_at in range(nyk):
                c = (yk_at // CORES * HALVES + zh_at) * CORES + yk_at % CORES
                place = (lane == lane_row + c * act_len) & (lane_row < act_len)
                gathered += dot(act_slots[zh_at, yk_at // CORES, yk_at % CORES], place.astype(f32).astype(bf16))

        loads[1].wait()
        embedded[...] = dot(gathered.astype(bf16), act_weight[...])

    pl.semaphore_wait(barrier, len(greeted))
    loads[0].wait()
    near_send, near_recv, _ = near_ring
    near_send(0)
    far_rings[0][0](0)
    far_y = []
    for d in range(1, ny):
        ref = block_at(far, z, y)
        far_y.append(push(ref, ref, dev_y(mod(y + d, ny))))
    loads[6].wait()
    act_pad[...] = jnp.zeros_like(act_pad)
    act_pad[0:seqs, 0:act_len] = act_raw[...].astype(f32)
    act_ring[z] = act_pad[...].astype(bf16)
    act_sem = {}

    def act_step(step):
        if step > 0:
            arrive(act_ring.at[mod(z - step, nz)], act_sem[step - 1])
        if step < nt:
            ref = act_ring.at[mod(z - step, nz)]
            act_sem[step] = push(ref, ref, dev_z(mod(z + 1, nz)))

    act_step(0)
    waiting = [spread_y(z)]
    rest = [far_rings[d] for d in near_first]
    owners_at = {}

    def lead_step(step):
        got = near_recv(step)
        if step + 1 < ring_steps:
            near_send(step + 1)
        owners_at[step] = far_rings[0][1](step)
        if step + 1 < ring_steps:
            far_rings[0][0](step + 1)
        act_step(step + 1)
        waiting.extend(spread_y(owner) for owner in got)

    def rest_step(step):
        owners = owners_at[step]
        for send, recv, _ in rest:
            got = recv(step)
            if step + 1 < ring_steps:
                send(step + 1)
            owners = got if len(got) > len(owners) else owners
        if step + 1 < ring_steps or steps_up == steps_down:
            shared_far.extend(share(far, owner) for owner in owners)
        else:
            shared_far.append(share(far, mod(z + ring_steps, nz)))

    def finish_waiting(count):
        for item in waiting[:count]:
            finish_near(*item)
        del waiting[:count]

    lead_step(0)
    for d in near_first:
        arrive(block_at(far, z, mod(y - d, ny)), far_y[d - 1])
        far_rings[d][0](0)
    shared_far.append(share(far, z))
    for step in range(ring_steps):
        if step + 1 < ring_steps:
            lead_step(step + 1)
        rest_step(step)
        if step + 2 == ring_steps:
            act_slots[zh, y, core] = act_ring[z]
            act_slots[1 - zh, y, core] = act_ring[mod(z - nt, nz)]
            for d in range(1, ny):
                ref = act_slots.at[:, y, core]
                act_sems.append(push(ref, ref, dev_y(mod(y + d, ny))))
        finish_waiting(1 if step == 0 else 2)
    for d in range(1, ny):
        arrive(act_slots.at[:, mod(y - d, ny), core], act_sems[d - 1])
    act_share = push(act_slots.at[:, :, core], act_slots.at[:, :, core], sibling)
    finish_waiting(len(waiting))
    arrive(act_slots.at[:, :, other], act_share)
    prepare_actions()

    def position(index):
        zh_at = lax.div(index, half)
        yk_at = lax.div(lax.rem(index, half), steps)
        c = (lax.div(yk_at, CORES) * HALVES + zh_at) * CORES + lax.rem(yk_at, CORES)
        return c * steps + lax.rem(index, steps)

    for load in loads[2:4] + loads[7:]:
        load.wait()
    lane_pos = position(iota((16, hist), 1))
    row_pos = position(iota((hist, 128), 0))

    last_f32[...] = jnp.zeros_like(last_f32)
    for dst, sem in shared_near + shared_far:
        arrive(dst, sem)
    for b in range(seqs):
        pick = (lane_pos == len_ref[b] - 1).astype(f32).astype(bf16)
        own = [dot(pick, rows_all[b, g].reshape(hist, feats)) for g in range(nt)]
        full = jnp.concatenate(own, axis=1)[0:1] + embedded[b : b + 1, :]
        last_f32[b : b + 1, :] = full
    last_rows = last_f32[...]
    last_round = last_rows.astype(bf16).astype(f32)
    last_bf[...] = jnp.concatenate([last_round, jnp.zeros_like(last_round)], axis=0).astype(bf16)
    loads[4].wait()
    query = dot(last_bf[...], weights[0])[0:8]
    row_id = iota((rows, inner), 0)
    row_head = lax.rem(row_id, heads) == lax.div(iota((rows, inner), 1), HEAD_DIM)

    def spread(x):
        out = jnp.zeros((rows, inner), f32)
        for b in range(seqs):
            out = jnp.where((lax.div(row_id, heads) == b) & row_head, x[b : b + 1, :], out)
        return out

    def fold(x):
        shape = x.shape
        seq_of = lax.div(iota(shape, 0), heads)
        out_row = iota((8, shape[1]), 0)
        out = jnp.zeros((8, shape[1]), f32)
        for b in range(seqs):
            total = jnp.sum(jnp.where(seq_of == b, x, 0.0), axis=0, keepdims=True)
            out = jnp.where(out_row == b, total, out)
        return out

    def per_seq(shape, make):
        seq_of = lax.div(iota(shape, 0), heads)
        out = jnp.zeros(shape, f32)
        for b in range(seqs):
            out = jnp.where(seq_of == b, make(b), out)
        return out

    query_rows = spread(query)
    key_vec = dot_split(query_rows, weights[1], NT_DIMS) * scale
    for g in range(nt):
        fact_a_src[g] = key_vec[:, g * feats : (g + 1) * feats].astype(bf16)
    fact_a[z] = fact_a_src[group]
    a_sems = {}
    for d in far_first:
        to = mod(z + d, nz)
        a_sems[d] = push(fact_a_src.at[lax.rem(to, nt)], fact_a.at[z], dev_z(to))

    def project(b):
        is_last = row_pos == len_ref[b] - 1
        mark = jnp.concatenate([is_last] * (feats // 128), axis=1)
        key_sum = jnp.zeros((hist, inner), f32)
        value_sum = jnp.zeros((hist, inner), f32)
        for g in range(nt):
            cut = slice(g * feats, (g + 1) * feats)
            block = rows_all[b, g].reshape(hist, feats).astype(f32)
            block = jnp.where(mark, last_round[b : b + 1, cut], block).astype(bf16)
            key_sum += dot(block, weights[1, cut, :])
            value_sum += dot(block, weights[2, cut, :])
        keys[b] = key_sum.astype(bf16)
        values[b] = value_sum.astype(bf16)

    for b in range(seqs):
        project(b)

    scores = per_seq((rows, hist), lambda b: dot_split(query_rows, keys[b], NT_DIMS)) * scale
    seq_row = lax.div(iota((rows, hist), 0), heads)
    pos = position(iota((rows, hist), 1))
    length = jnp.zeros((rows, hist), jnp.int32)
    for b in range(seqs):
        length = jnp.where(seq_row == b, len_ref[b], length)
    scores = jnp.where(pos < length, scores, -1e30)
    weight = jnp.exp(scores - jnp.max(scores, axis=1, keepdims=True))
    weight = jnp.where(pos < length, weight, 0.0)
    attention = weight / jnp.sum(weight, axis=1, keepdims=True)
    attention_round = attention.astype(bf16)
    attended = per_seq((rows, inner), lambda b: dot(attention_round, values[b]))
    attended = fold(jnp.where(row_head, attended, 0.0))
    loads[5].wait()
    attended_bf = jnp.concatenate([attended, jnp.zeros_like(attended)], axis=0).astype(bf16)
    head_part = dot(attended_bf, out_weight[...])
    quarter = width // 4
    hid_slots[group] = jnp.concatenate(
        [head_part[0:seqs, j * quarter : (j + 1) * quarter] for j in range(4)], axis=0
    ).astype(bf16)
    hid_sems = []
    for d in range(1, nt):
        to = mod(group + d, nt)
        hid_sems.append(push(hid_slots.at[group], hid_slots.at[group], dev_z(zh * nt + to)))

    for h in range(HALVES):
        fact_c_src[h] = attention_round[:, h * half : (h + 1) * half]
    fact_c[z] = fact_c_src[zh]
    c_sems = {}
    for d in far_first:
        to = mod(z + d, nz)
        c_sems[d] = push(fact_c_src.at[lax.div(to, nt)], fact_c.at[z], dev_z(to))

    for d in range(1, nz):
        arrive(fact_a.at[mod(z - d, nz)], a_sems[d])
    for d in range(1, nt):
        arrive(hid_slots.at[mod(group - d, nt)], hid_sems[d - 1])
    total = hid_slots[0].astype(f32)
    for g in range(1, nt):
        total = total + hid_slots[g].astype(f32)
    zero_rows = jnp.zeros((8 - seqs, width), f32)
    head_sum = jnp.concatenate([total[j * seqs : (j + 1) * seqs] for j in range(4)], axis=1)
    hidden = last_rows + jnp.concatenate([head_sum, zero_rows], axis=0)
    gain_head = gain_ref[...] * head_ref[...]
    inverse = lax.rsqrt(jnp.sum(hidden * hidden, axis=1, keepdims=True) * (1.0 / width) + NORM_EPS)
    normed = hidden * inverse
    q_vals = jnp.sum(gain_head * normed, axis=1, keepdims=True)
    q_lane = iota((8, 128), 1)
    q_row = iota((8, 128), 0)
    q_line = jnp.sum(jnp.where(q_lane == q_row, q_vals, 0.0), axis=0, keepdims=True)
    boot = jnp.zeros((8, 1), f32)
    for b in range(seqs):
        boot = jnp.where(iota((8, 1), 0) == b, boot_ref[0, b].astype(f32), boot)
    grad_normed = boot * gain_head
    mean = jnp.sum(grad_normed * normed, axis=1, keepdims=True) * (1.0 / width)
    grad_last = inverse * (grad_normed - normed * mean)

    grad_heads = spread(dot_split(grad_last, out_weight[...], NT_DIMS))
    value_vec = dot_split(grad_heads, weights[2], NT_DIMS)
    before_b = len(sends)
    for g in range(nt):
        fact_b_src[g] = value_vec[:, g * feats : (g + 1) * feats].astype(bf16)
    fact_b[z] = fact_b_src[group]
    b_sems = {}
    for d in far_first:
        to = mod(z + d, nz)
        b_sems[d] = push(fact_b_src.at[lax.rem(to, nt)], fact_b.at[z], dev_z(to))
    grad_attention = per_seq((rows, hist), lambda b: dot_split(grad_heads, values[b], NT_DIMS))
    grad_scores = attention * (
        grad_attention - jnp.sum(attention * grad_attention, axis=1, keepdims=True)
    )
    for h in range(HALVES):
        fact_d_src[h] = grad_scores[:, h * half : (h + 1) * half].astype(bf16)
    fact_d[z] = fact_d_src[zh]
    d_sems = {}
    for d in far_first:
        to = mod(z + d, nz)
        d_sems[d] = push(fact_d_src.at[lax.div(to, nt)], fact_d.at[z], dev_z(to))

    grad_query = per_seq((rows, inner), lambda b: dot_split(grad_scores, keys[b]))
    grad_query = fold(jnp.where(row_head, grad_query, 0.0)) * scale
    from_query = dot_split(grad_query, weights[0], NT_DIMS)
    extra_rows = from_query + jnp.where(group == 0, 1.0, 0.0) * grad_last
    at_last = pos == length - 1
    score_last = jnp.sum(jnp.where(at_last, grad_scores, 0.0), axis=1, keepdims=True)
    weight_last = jnp.sum(
        jnp.where(at_last, attention_round.astype(f32), 0.0), axis=1, keepdims=True
    )
    grad_lastrow = extra_rows + fold(score_last * key_vec + weight_last * value_vec)
    act_terms = dot_split(grad_lastrow, act_weight[...], NT_DIMS)
    act_cols = dot_exact(act_terms, act_pick[...])
    cut = feats // 2
    for z_at in range(nz):
        g = z_at % nt
        extra_src[z_at, 0:seqs, :cut] = extra_rows[0:seqs, g * feats : g * feats + cut]
        extra_src[z_at, seqs : 2 * seqs, :cut] = extra_rows[0:seqs, g * feats + cut : (g + 1) * feats]
        extra_src[z_at, :, cut:] = act_cols[:, z_at * 128 : (z_at + 1) * 128]
    extra[z] = extra_src[z]
    x_sems = {}
    for d in far_first:
        to = mod(z + d, nz)
        x_sems[d] = (push(extra_src.at[to], extra.at[z], dev_z(to)))

    drain(before_b)
    factors = nz * rows
    for d in range(1, nz):
        arrive(fact_c.at[mod(z - d, nz)], c_sems[d])
    coef_b = fact_c[...].reshape(factors, half).astype(f32).T
    for d in range(1, nz):
        arrive(fact_b.at[mod(z - d, nz)], b_sems[d])
        arrive(fact_d.at[mod(z - d, nz)], d_sems[d])
    coef_a = fact_d[...].reshape(factors, half).astype(f32).T
    coefs = jnp.concatenate([coef_a, coef_b], axis=1)
    vecs = jnp.concatenate(
        [fact_a[...].reshape(factors, feats), fact_b[...].reshape(factors, feats)], axis=0
    )
    seq_col = lax.div(lax.rem(iota(coefs.shape, 1), rows), heads)
    y_sems = {}
    sib_sems = {}

    def multiply(b):
        out = dot(jnp.where(seq_col == b, coefs, 0.0).astype(bf16), vecs)
        partial[b] = out.reshape(ny, CORES, steps, feats)
        sib_sems[b] = push(partial.at[b, :, other], sib_part.at[b], sibling)

    def over_y(b):
        arrive(sib_part.at[b], sib_sems[b])
        total = partial[b, :, core] + sib_part[b]
        row_sum[b] = total
        row_send[b] = total.astype(bf16)
        for d in range(1, ny):
            y_sems[b, d] = push(
                row_send.at[b, mod(y + d, ny)], row_parts.at[d - 1, b], dev_y(mod(y + d, ny))
            )

    multiply(0)
    multiply(1)
    over_y(0)
    multiply(2)
    over_y(1)
    for d in range(1, nz):
        arrive(extra.at[mod(z - d, nz)], x_sems[d])
    extra_sum = extra[0]
    for z_at in range(1, nz):
        extra_sum = extra_sum + extra[z_at]
    act_sum[yk] = extra_sum
    act_sems = []
    for d in range(1, nyk):
        act_sems.append(push(act_sum.at[yk], act_sum.at[yk], dev_yk(mod(yk + d, nyk))))
    multiply(3)
    over_y(2)
    over_y(3)
    drain(3 * (nz - 1))

    for d in range(1, nyk):
        arrive(act_sum.at[mod(yk - d, nyk)], act_sems[d - 1])
    act_total = act_sum[0]
    for yk_at in range(1, nyk):
        act_total = act_total + act_sum[yk_at]
    mine = (iota((128, 128), 0) == iota((128, 128), 1) + yk * part) & (iota((128, 128), 1) < part)
    act_mine = dot_exact(act_total[:, cut:], mine.astype(f32).astype(bf16))
    out_ref[seqs * steps :, 0:128] = jnp.where(iota((8, 128), 0) == 0, q_line, 0.0)
    out_ref[seqs * steps :, 128:256] = act_mine
    here = iota((steps, feats), 0) + critic * steps
    for b in range(seqs):
        low = jnp.concatenate([act_total[b : b + 1, :cut], act_total[seqs + b : seqs + b + 1, :cut]], axis=1)
        result = row_sum[b, y] + jnp.where(here == len_ref[b] - 1, low, 0.0)
        for d in range(1, ny):
            arrive(row_parts.at[d - 1, b], y_sems[b, d])
            result = result + row_parts[d - 1, b].astype(f32)
        out_ref[b * steps : (b + 1) * steps, :] = result
    drain(len(sends))


def unpack(packed, q_ref, grad_ref, actgrad_ref):
    seqs, steps, feats = grad_ref.shape
    tail = seqs * steps
    q_ref[...] = packed[tail : tail + 1, 0:seqs]
    grad_ref[...] = packed[0:tail, :].reshape(seqs, steps, feats)
    actgrad_ref[...] = packed[tail : tail + seqs, 128 : 128 + actgrad_ref.shape[1]]


def solution(mesh):
    nt = mesh.shape["tensor"]
    ny = mesh.shape["critic"] // (HALVES * CORES)
    nz = HALVES * nt
    nyk = ny * CORES

    def on_device(obs, actions, lengths, boot, project, out_weight, act_weight, gain, head):
        seqs, steps, feats = obs.shape
        width, inner = project.shape[1], project.shape[3]
        act_len = actions.shape[1]
        rows = seqs * (inner // HEAD_DIM)
        hist = steps * HALVES * nyk
        half = steps * nyk
        weights = jnp.transpose(project[0], (1, 0, 2))
        vmem = pl.BlockSpec(memory_space=pltpu.VMEM)
        hbm = pl.BlockSpec(memory_space=pltpu.HBM)
        part = act_len // nt
        flops = 4 * seqs * hist * width * inner
        packed = pl.pallas_call(
            functools.partial(kernel, (ny, nt, seqs, steps, feats, inner, act_len)),
            out_shape=jax.ShapeDtypeStruct((seqs * steps + 8, feats), f32),
            in_specs=[hbm] * 9,
            out_specs=vmem,
            scratch_shapes=[
                pltpu.VMEM((seqs, nt, HALVES, ny, CORES, steps, feats), bf16),
                pltpu.VMEM((3, width, inner), bf16),
                pltpu.VMEM((inner, width), bf16),
                pltpu.VMEM(act_weight.shape[1:], bf16),
                pltpu.VMEM((nz, 16, 128), bf16),
                pltpu.VMEM((HALVES, ny, CORES, 16, 128), bf16),
                pltpu.VMEM((seqs, hist, inner), bf16),
                pltpu.VMEM((seqs, hist, inner), bf16),
                pltpu.VMEM((16, width), f32),
                pltpu.VMEM((8, width), f32),
                pltpu.VMEM((16, width), bf16),
                pltpu.VMEM((nt, 16, width // 4), bf16),
                pltpu.VMEM((nt, rows, feats), bf16),
                pltpu.VMEM((nz, rows, feats), bf16),
                pltpu.VMEM((HALVES, rows, half), bf16),
                pltpu.VMEM((nz, rows, half), bf16),
                pltpu.VMEM((nt, rows, feats), bf16),
                pltpu.VMEM((nz, rows, feats), bf16),
                pltpu.VMEM((HALVES, rows, half), bf16),
                pltpu.VMEM((nz, rows, half), bf16),
                pltpu.VMEM((nz, 8, feats // 2 + 128), f32),
                pltpu.VMEM((nz, 8, feats // 2 + 128), f32),
                pltpu.VMEM((seqs, ny, CORES, steps, feats), f32),
                pltpu.VMEM((seqs, ny, steps, feats), f32),
                pltpu.VMEM((seqs, ny, steps, feats), f32),
                pltpu.VMEM((seqs, ny, steps, feats), bf16),
                pltpu.VMEM((ny - 1, seqs, steps, feats), bf16),
                pltpu.VMEM((act_weight.shape[1], nz * 128), bf16),
                pltpu.VMEM((nyk, 8, feats // 2 + 128), f32),
                pltpu.VMEM((seqs, act_len), bf16),
                pltpu.VMEM((16, 128), f32),
                pltpu.SMEM((seqs,), jnp.int32),
                pltpu.SMEM((1, seqs), jnp.int32),
                pltpu.VMEM((1, width), f32),
                pltpu.VMEM((1, width), f32),
                pltpu.SemaphoreType.DMA((11,)),
                pltpu.SemaphoreType.DMA((160,)),
                pltpu.SemaphoreType.DMA((160,)),
            ],
            compiler_params=pltpu.CompilerParams(
                collective_id=0, has_side_effects=True, vmem_limit_bytes=63 * 1024 * 1024
            ),
            cost_estimate=pl.CostEstimate(
                flops=flops, bytes_accessed=10 * 1024 * 1024, transcendentals=seqs * hist
            ),
        )(obs, actions, lengths, boot, weights, out_weight[0], act_weight[0], gain, head)
        return pl.pallas_call(
            unpack,
            out_shape=(
                jax.ShapeDtypeStruct((1, seqs), f32),
                jax.ShapeDtypeStruct((seqs, steps, feats), f32),
                jax.ShapeDtypeStruct((seqs, part), f32),
            ),
            in_specs=[vmem],
            out_specs=(vmem, vmem, vmem),
        )(packed)

    in_specs = (
        P("seq", "critic", "tensor"),
        P("seq", "critic"),
        P("seq"),
        P("critic", "seq"),
        P("critic", None, None, "tensor"),
        P("critic", "tensor", None),
        P("critic", None, None),
        P("critic", None),
        P("critic", None),
    )
    out_specs = (P("critic", "seq"), P("seq", "critic", "tensor"), P("seq", ("critic", "tensor")))
    return jax.shard_map(
        on_device, mesh=mesh, in_specs=in_specs, out_specs=out_specs, check_vma=False
    )
```
